128 devices in a mesh: row: 16 (over y, z), col: 8 (over x, core).
Axes of the slice: x: 4, y: 4, z: 4, core: 2. Of those that a mesh axis runs over, the one named last changes fastest.
Arguments:
- sigma_root: float32 [4096, 4096], P('row', 'col')
- first_panel: float32 [4096, 4096], P('row', 'col'), may hold values from -0.1875 to 0.1875
- first_pivots: float32 [2048, 4096], P('row', 'col')
- second_root_panel: float32 [4096, 4096], P('row', 'col'), may hold values from -0.15625 to 0.15625
- second_parent_panel: float32 [2048, 4096], P('row', 'col'), may hold values from -0.15625 to 0.15625
- second_pivots: float32 [1024, 4096], P('row', 'col')
- first_flags: int32 [2, 16], replicated, may hold values from 0 to 1, as said below
- second_flags: int32 [4, 24], replicated, may hold values from 0 to 1, as said below
Outputs:
- first_sigma: float32 [4096, 4096], P('row', 'col')
- first_diagonal: float32 [2048, 4096], P('row', 'col')
- second_root: float32 [4096, 4096], P('row', 'col')
- second_parent: float32 [2048, 4096], P('row', 'col')
- second_diagonal: float32 [1024, 4096], P('row', 'col')
The draws below stay inside these ranges and needn't reach their ends.
Inputs may be any that keep to these rules, and one draw needn't show every extreme that they name: first_flags[n, b] is 1 where block row b of the root lies in the structure of level-one node n, else 0. second_flags[m, b] is 1 where block b (the 4096 // 256 root blocks, then the 8 blocks of the parent m // 2) lies in the structure of level-two node m, else 0; a root block in the structure of node m is in the structure of its parent m // 2.
All inputs are finite; a program needn't handle non-finite values.
Results may differ from the reference program's by a relative error of at most 0.0001.
Values sent between devices are 32-bit elements; how exact they have to be, the bound alone decides.
A program may use at most 128 MiB of HBM per device.

```python
import math
import jax
import jax.numpy as jnp
from jax import lax

BLOCK_SIZE = 256
ROOT_ORDER = 4096
FIRST_ORDER = 2048
SECOND_ORDER = 1024


def symmetric_blocks(key, blocks_count, order):
    noise = jax.random.normal(jax.random.fold_in(key, 21), (blocks_count, order, order), jnp.float32)
    paired = (noise + jnp.swapaxes(noise, 1, 2)) * (0.5 / math.sqrt(2.0 * order))
    diagonal = jax.random.uniform(jax.random.fold_in(key, 22), (blocks_count, order), jnp.float32, 1.5, 3.0)
    identity = jnp.eye(order, dtype=jnp.float32)
    matrices = paired * (1.0 - identity) + identity * diagonal[:, :, None]
    return jnp.swapaxes(matrices, 0, 1).reshape(order, blocks_count * order)


def structure_draw(key):
    root_blocks = ROOT_ORDER // BLOCK_SIZE
    parent_blocks = FIRST_ORDER // BLOCK_SIZE
    first_table = (jax.random.randint(jax.random.fold_in(key, 11), (2, root_blocks), 0, 10) < 6).astype(jnp.int32)
    inherit = (jax.random.randint(jax.random.fold_in(key, 12), (4, root_blocks), 0, 10) < 7).astype(jnp.int32)
    own_blocks = (jax.random.randint(jax.random.fold_in(key, 13), (4, parent_blocks), 0, 10) < 7).astype(jnp.int32)
    parents = jnp.repeat(first_table, 2, axis=0)
    second_table = jnp.concatenate([parents * inherit, own_blocks], axis=1)
    return (first_table, second_table)


def draw_sigma_root(key, part):
    key = jax.random.fold_in(key, 1)
    return symmetric_blocks(key, 1, ROOT_ORDER)


def draw_first_pivots(key, part):
    key = jax.random.fold_in(key, 2)
    return symmetric_blocks(key, 2, FIRST_ORDER)


def draw_second_pivots(key, part):
    key = jax.random.fold_in(key, 3)
    return symmetric_blocks(key, 4, SECOND_ORDER)


def draw_first_flags(key, part):
    shared = structure_draw(key)
    return shared[0]


def draw_second_flags(key, part):
    shared = structure_draw(key)
    return shared[1]


def block_scale(stream_key, shape, cuts, smallest, largest):
    def one(axis_at, parts):
        steps = jax.random.uniform(jax.random.fold_in(jax.random.fold_in(stream_key, 6), axis_at), (parts,), jnp.float32, smallest / len(cuts), largest / len(cuts))
        return jnp.repeat(jnp.exp(steps), shape[axis_at] // parts).reshape((-1,) + (1,) * (len(shape) - axis_at - 1))

    gain = one(*cuts[0])
    for cut in cuts[1:]:
        gain = gain * one(*cut)
    return gain


def bell_draw(stream_key, shape, scale, most, cuts=(), kind=jnp.bfloat16):
    values = scale * jax.random.normal(stream_key, shape, jnp.float32)
    if cuts:
        values = values * block_scale(stream_key, shape, cuts, -0.22, 0.18)
    return jnp.clip(values, -most, most).astype(kind)


def setup_inputs(seed: int = 0) -> dict:
    splits = jax.random.split(jax.random.key(seed), 9)
    return {
        "sigma_root": draw_sigma_root(jax.random.fold_in(splits[8], 71), 0),
        "first_panel": bell_draw(splits[1], (ROOT_ORDER, 2 * FIRST_ORDER), (ROOT_ORDER // 4) ** -0.5, 0.1875, ((0, 16), (1, 8)), jnp.float32),
        "first_pivots": draw_first_pivots(jax.random.fold_in(splits[8], 71), 0),
        "second_root_panel": bell_draw(splits[3], (ROOT_ORDER, 4 * SECOND_ORDER), ((ROOT_ORDER + FIRST_ORDER) // 4) ** -0.5, 0.15625, ((0, 16), (1, 8)), jnp.float32),
        "second_parent_panel": bell_draw(splits[4], (FIRST_ORDER, 4 * SECOND_ORDER), ((ROOT_ORDER + FIRST_ORDER) // 4) ** -0.5, 0.15625, ((0, 16), (1, 8)), jnp.float32),
        "second_pivots": draw_second_pivots(jax.random.fold_in(splits[8], 71), 0),
        "first_flags": draw_first_flags(jax.random.fold_in(splits[8], 71), 0),
        "second_flags": draw_second_flags(jax.random.fold_in(splits[8], 71), 0),
    }


def product(left_side, right_side):
    return jnp.dot(left_side, right_side, precision=lax.Precision.HIGHEST, preferred_element_type=jnp.float32)


def expand(flag_table):
    return jnp.repeat(flag_table.astype(jnp.float32), BLOCK_SIZE, axis=1)


def reference(sigma_root, first_panel, first_pivots, second_root_panel, second_parent_panel, second_pivots, first_flags, second_flags):
    first_rows = expand(first_flags)
    second_rows = expand(second_flags)
    first_blocks = []
    first_diagonals = []
    for node_index in range(2):
        columns = slice(node_index * FIRST_ORDER, (node_index + 1) * FIRST_ORDER)
        row_mask = first_rows[node_index][:, None]
        lowered = first_panel[:, columns] * row_mask
        result_block = -row_mask * product(sigma_root, lowered)
        first_blocks.append(result_block)
        first_diagonals.append(first_pivots[:, columns] - product(lowered.T, result_block))
    first_sigma = jnp.concatenate(first_blocks, axis=1)
    first_diagonal = jnp.concatenate(first_diagonals, axis=1)
    root_blocks = []
    parent_blocks = []
    second_diagonals = []
    for node_index in range(4):
        parent_index = node_index // 2
        columns = slice(node_index * SECOND_ORDER, (node_index + 1) * SECOND_ORDER)
        parent_columns = slice(parent_index * FIRST_ORDER, (parent_index + 1) * FIRST_ORDER)
        root_mask = second_rows[node_index, :ROOT_ORDER][:, None]
        parent_mask = second_rows[node_index, ROOT_ORDER:][:, None]
        root_lower = second_root_panel[:, columns] * root_mask
        parent_lower = second_parent_panel[:, columns] * parent_mask
        crossing = first_sigma[:, parent_columns]
        root_inner = product(sigma_root, root_lower) + product(crossing, parent_lower)
        parent_inner = product(crossing.T, root_lower) + product(first_diagonal[:, parent_columns], parent_lower)
        root_result = -root_mask * root_inner
        parent_result = -parent_mask * parent_inner
        root_blocks.append(root_result)
        parent_blocks.append(parent_result)
        second_diagonals.append(second_pivots[:, columns] - product(root_lower.T, root_result) - product(parent_lower.T, parent_result))
    return (first_sigma, first_diagonal, jnp.concatenate(root_blocks, axis=1), jnp.concatenate(parent_blocks, axis=1), jnp.concatenate(second_diagonals, axis=1))
```

```python
import jax
import jax.numpy as jnp
from jax import lax
from jax.experimental import pallas as pl
from jax.experimental.pallas import tpu as pltpu
from jax.sharding import PartitionSpec as P

MESH = pl.DeviceIdType.MESH
F32 = jnp.float32
BF16 = jnp.bfloat16
RING = 4
COPIES = 80


def split(value):
    high = value.astype(BF16)
    low = (value - high.astype(F32)).astype(BF16)
    return high, low


def dot3(left, right):
    (lh, ll), (rh, rl) = left, right
    total = jnp.dot(lh, rh, preferred_element_type=F32)
    total += jnp.dot(lh, rl, preferred_element_type=F32)
    total += jnp.dot(ll, rh, preferred_element_type=F32)
    return total


class Copies:
    def __init__(self, send_sems, recv_sems):
        self.send_sems, self.recv_sems = send_sems, recv_sems
        self.count = 0
        self.started = []

    def make(self, src, dst, device):
        number = self.count
        self.count += 1
        return pltpu.make_async_remote_copy(
            src_ref=src,
            dst_ref=dst,
            send_sem=self.send_sems.at[number],
            recv_sem=self.recv_sems.at[number],
            device_id=device,
            device_id_type=MESH,
        )

    def start(self, src, dst, device):
        copy = self.make(src, dst, device)
        copy.start()
        self.started.append(copy)
        return copy

    def finish(self):
        for copy in self.started:
            copy.wait_send()


class Gather:
    def __init__(self, copies, plus, minus, index, piece, halves):
        self.copies, self.plus, self.minus = copies, plus, minus
        self.index, self.piece, self.halves = index, piece, halves

    def first(self):
        own = self.piece(self.index)
        self.from_minus = self.copies.start(own, own, self.plus)
        self.from_plus = self.copies.start(own, own, self.minus)

    def second(self):
        self.from_minus.wait_recv()
        half = self.halves((self.index + 3) % RING)[0]
        self.low = self.copies.start(half, half, self.plus)
        self.from_plus.wait_recv()
        half = self.halves((self.index + 1) % RING)[1]
        self.high = self.copies.start(half, half, self.minus)

    def third(self):
        self.low.wait_recv()
        self.high.wait_recv()


class Scatter:
    def __init__(self, copies, plus, minus, index, piece, halves, half_in, full_in):
        self.copies, self.plus, self.minus = copies, plus, minus
        self.index, self.piece, self.halves = index, piece, halves
        self.half_in, self.full_in = half_in, full_in

    def first(self):
        low, high = self.halves((self.index + 2) % RING)
        self.low = self.copies.start(low, self.half_in.at[0], self.plus)
        self.high = self.copies.start(high, self.half_in.at[1], self.minus)

    def second(self):
        target = (self.index + 1) % RING
        half = self.halves(target)[0]
        self.low.wait_recv()
        half[...] = half[...] + self.half_in[0]
        self.from_minus = self.copies.start(self.piece(target), self.full_in.at[0], self.plus)
        target = (self.index + 3) % RING
        half = self.halves(target)[1]
        self.high.wait_recv()
        half[...] = half[...] + self.half_in[1]
        self.from_plus = self.copies.start(self.piece(target), self.full_in.at[1], self.minus)

    def third(self):
        self.from_minus.wait_recv()
        self.from_plus.wait_recv()
        return self.piece(self.index)[...] + self.full_in[0] + self.full_in[1]


class Group:
    def __init__(self, copies, chip, core, index, buffer):
        self.copies, self.chip, self.core = copies, chip, core
        self.index, self.buffer = index, buffer

    def first(self):
        own = self.buffer.at[self.index]
        self.from_chip = self.copies.start(own, own, self.chip)
        self.from_core = self.copies.start(own, own, self.core)

    def second(self):
        self.from_chip.wait_recv()
        other = self.buffer.at[(self.index + 2) % RING]
        self.onward = self.copies.start(other, other, self.core)

    def third(self):
        self.from_core.wait_recv()
        self.onward.wait_recv()


def kernel(
    first_flags,
    second_flags,
    sigma,
    panel,
    pivots,
    root_panel,
    parent_panel,
    second_pivots,
    out_sigma,
    out_diag,
    out_root,
    out_parent,
    out_second,
    turned,
    blocks,
    low_group,
    pivot_group,
    parent_all,
    parent_pair,
    lower,
    reduced,
    reduced_pair,
    lower_high,
    lower_low,
    red_high,
    red_low,
    product_a,
    half_a,
    full_a,
    product_b,
    half_b,
    full_b,
    cross_turned,
    cross_group,
    product_c,
    half_c,
    full_c,
    pivot_parent,
    diag_sum,
    half_d0,
    full_d0,
    half_d1,
    full_d1,
    half_e0,
    full_e0,
    half_e1,
    full_e1,
    send_sems,
    recv_sems,
    local_sems,
):
    row = lax.axis_index("row")
    col = lax.axis_index("col")
    y, z = row // RING, row % RING
    x, core = col // 2, col % 2
    local = col % RING

    def device(at_x, at_core, at_y, at_z):
        return (at_y * RING + at_z, at_x * 2 + at_core)

    z_plus = device(x, core, y, (z + 1) % RING)
    z_minus = device(x, core, y, (z + 3) % RING)
    y_plus = device(x, core, (y + 1) % RING, z)
    y_minus = device(x, core, (y + 3) % RING, z)
    x_plus = device((x + 1) % RING, core, y, z)
    x_minus = device((x + 3) % RING, core, y, z)
    x_pair = device(x + 1 - 2 * (x % 2), core, y, z)
    other_core = device(x, 1 - core, y, z)

    barrier = pltpu.get_barrier_semaphore()
    friends = [y_plus, y_minus, x_plus, x_minus]
    for step in range(RING):
        for flip in range(2):
            if step or flip:
                friends.append(device(x, (core + flip) % 2, y, (z + step) % RING))
    for friend in friends:
        pl.semaphore_signal(barrier, inc=1, device_id=friend, device_id_type=MESH)
    first_flag = first_flags[col // RING, row].astype(F32)
    root_flag = second_flags[x, row].astype(F32)
    parent_flag = second_flags[x, RING * RING + row // 2].astype(F32)
    parent_lower = parent_panel[...] * parent_flag
    parent_all[y, z] = parent_lower
    parent_pair[core] = parent_lower
    turned[0] = sigma[:, 0:256].T
    turned[1] = sigma[:, 256:512].T
    masked = panel[...] * first_flag
    lower[z] = masked
    low_group[local] = masked
    pivot_group[local] = pivots[...]
    pl.semaphore_wait(barrier, len(friends))

    copies = Copies(send_sems, recv_sems)

    parent_y0 = Gather(
        copies, y_plus, y_minus, y,
        lambda i: parent_all.at[i, z, 0:64],
        lambda i: (parent_all.at[i, z, 0:32], parent_all.at[i, z, 32:64]),
    )
    parent_z1 = Gather(
        copies, z_plus, z_minus, z,
        lambda i: parent_all.at[y, i, 64:128],
        lambda i: (parent_all.at[y, i, 64:96], parent_all.at[y, i, 96:128]),
    )
    parent_z0 = Gather(
        copies, z_plus, z_minus, z,
        lambda i: parent_all.at[:, i, 0:64],
        lambda i: (parent_all.at[0:2, i, 0:64], parent_all.at[2:4, i, 0:64]),
    )
    parent_y1 = Gather(
        copies, y_plus, y_minus, y,
        lambda i: parent_all.at[i, :, 64:128],
        lambda i: (parent_all.at[i, 0:2, 64:128], parent_all.at[i, 2:4, 64:128]),
    )
    parent_y0.first()
    parent_z1.first()

    sigma_send = []
    for j in range(2):
        at_z = core * 2 + j
        number = copies.count
        copies.count += 1
        copy = pltpu.make_async_remote_copy(
            src_ref=turned.at[j],
            dst_ref=blocks.at[x, z],
            send_sem=send_sems.at[number],
            recv_sem=local_sems.at[z % 2],
            device_id=device(x, z // 2, y, at_z),
            device_id_type=MESH,
        )
        sigma_send.append((at_z, copy))

        @pl.when(at_z != z)
        def _():
            copy.start()

        @pl.when(at_z == z)
        def _():
            blocks[x, z] = turned[j]

    low_gather = Group(copies, x_pair, other_core, local, low_group)
    low_gather.first()
    lower_gather = Gather(
        copies, z_plus, z_minus, z,
        lambda i: lower.at[i],
        lambda i: (lower.at[i, 0:128], lower.at[i, 128:256]),
    )
    lower_gather.first()
    pair = parent_pair.at[core]
    pair_copy = copies.start(pair, pair, other_core)

    for j in range(2):
        from_z = core * 2 + j

        @pl.when(from_z != z)
        def _():
            pltpu.make_async_remote_copy(
                src_ref=turned.at[j],
                dst_ref=blocks.at[x, from_z],
                send_sem=send_sems.at[0],
                recv_sem=local_sems.at[j],
                device_id=other_core,
                device_id_type=MESH,
            ).wait_recv()

    sigma_gather = Gather(
        copies, x_plus, x_minus, x,
        lambda i: blocks.at[i, pl.ds(2 * core, 2)],
        lambda i: (blocks.at[i, 2 * core], blocks.at[i, 2 * core + 1]),
    )
    sigma_gather.first()

    def share(i):
        ref = blocks.at[i, pl.ds(2 * core, 2)]
        return copies.start(ref, ref, other_core)

    sigma_core = [share(x)]
    parent_y0.second()
    parent_z1.second()
    low_gather.second()
    pivot_gather = Group(copies, x_pair, other_core, local, pivot_group)
    pivot_gather.first()
    parent_y0.third()
    parent_z0.first()
    parent_z1.third()
    parent_y1.first()
    lower_gather.second()
    sigma_gather.second()
    sigma_core.append(share((x + 1) % RING))
    sigma_core.append(share((x + 3) % RING))
    parent_z0.second()
    parent_y1.second()
    pivot_gather.second()
    low_gather.third()
    parent_z0.third()
    parent_y1.third()

    total = root_panel[...] * root_flag
    for i in range(RING):
        total -= dot3(split(low_group[i]), split(parent_all[i].reshape(512, 512)))
    reduced[z] = total
    reduced_pair[core] = total
    reduced_gather = Gather(
        copies, z_plus, z_minus, z,
        lambda i: reduced.at[i],
        lambda i: (reduced.at[i, 0:128], reduced.at[i, 128:256]),
    )
    reduced_gather.first()
    ref = reduced_pair.at[core]
    reduced_copy = copies.start(ref, ref, other_core)

    lower_gather.third()
    sigma_gather.third()
    sigma_core.append(share((x + 2) % RING))
    for i in range(RING):
        high, low = split(lower[i])
        lower_high[i] = high
        lower_low[i] = low
    for copy in sigma_core:
        copy.wait_recv()

    def product(at, high, low):
        total = None
        for i in range(RING):
            term = dot3(split(blocks[at, i]), (high[i], low[i]))
            total = term if total is None else total + term
        return total

    def root_scatter(summed, half_in, full_in):
        return Scatter(
            copies, y_plus, y_minus, y,
            lambda i: summed.at[i],
            lambda i: (summed.at[i, 0:128], summed.at[i, 128:256]),
            half_in, full_in,
        )

    def fill(into, at, high, low):
        into[at] = product(at, high, low)

    scatter_a = root_scatter(product_a, half_a, full_a)
    at = (y + 2) % RING
    fill(product_a, at, lower_high, lower_low)
    scatter_a.first()
    reduced_gather.second()
    for step in (1, 3):
        fill(product_a, (y + step) % RING, lower_high, lower_low)
    scatter_a.second()
    fill(product_a, y, lower_high, lower_low)
    reduced_gather.third()
    for i in range(RING):
        high, low = split(reduced[i])
        red_high[i] = high
        red_low[i] = low
    scatter_b = root_scatter(product_b, half_b, full_b)
    fill(product_b, (y + 2) % RING, red_high, red_low)
    cross = scatter_a.third() * (-first_flag)
    scatter_b.first()
    out_sigma[...] = cross
    cross_turned[...] = cross.T.reshape(RING, 128, 256)

    cross_group[local, z] = cross_turned[z]
    cross_copies = []
    for step in (1, 3, 2):
        at_z = (z + step) % RING
        cross_copies.append(
            copies.start(
                cross_turned.at[at_z],
                cross_group.at[local, z],
                device(x, core, y, at_z),
            )
        )
    for step in (1, 3):
        fill(product_b, (y + step) % RING, red_high, red_low)
    scatter_b.second()
    for copy in cross_copies:
        copy.wait_recv()
    cross_gather = Group(copies, x_pair, other_core, local, cross_group)
    cross_gather.first()
    fill(product_b, y, red_high, red_low)

    pivot_gather.third()
    pair_copy.wait_recv()
    total = jnp.zeros((128, 512), F32)
    for i in range(RING):
        total += dot3(split(pivot_group[i]), split(parent_all[i].reshape(512, 512)))
    pivot_parent[...] = total
    right = split(total)
    for k in range(2):
        term = dot3(split(parent_pair[k].T), right)
        diag_sum[2 * k : 2 * k + 2] = term.reshape(2, RING, 64, 512)
    cross_gather.second()

    result = scatter_b.third()
    out_root[...] = result * (-root_flag)
    reduced_copy.wait_recv()
    right = split(result)
    for k in range(2):
        term = dot3(split(reduced_pair[k].T), right)
        diag_sum[2 * k : 2 * k + 2] += term.reshape(2, RING, 64, 512)
    diag_y0 = Scatter(
        copies, y_plus, y_minus, y,
        lambda i: diag_sum.at[i, :, :, 0:256],
        lambda i: (diag_sum.at[i, 0:2, :, 0:256], diag_sum.at[i, 2:4, :, 0:256]),
        half_d0, full_d0,
    )
    diag_z1 = Scatter(
        copies, z_plus, z_minus, z,
        lambda i: diag_sum.at[:, i, :, 256:512],
        lambda i: (diag_sum.at[0:2, i, :, 256:512], diag_sum.at[2:4, i, :, 256:512]),
        half_d1, full_d1,
    )
    diag_y0.first()
    diag_z1.first()
    cross_gather.third()

    def node_fill(at):
        first, second = None, None
        for i in range(RING):
            left = split(cross_group[at, i])
            term = dot3(left, (lower_high[i], lower_low[i]))
            first = term if first is None else first + term
            term = dot3(left, (red_high[i], red_low[i]))
            second = term if second is None else second + term
        product_c[at, 0] = first
        product_c[at, 1] = second

    scatter_c = Scatter(
        copies, y_plus, y_minus, y,
        lambda i: product_c.at[i],
        lambda i: (product_c.at[i, 0], product_c.at[i, 1]),
        half_c, full_c,
    )
    node_fill((y + 2) % RING)
    scatter_c.first()
    diag_y0.second()
    diag_z1.second()
    for step in (1, 3):
        node_fill((y + step) % RING)
    scatter_c.second()
    node_fill(y)
    diag_sum[y, :, :, 0:256] = diag_y0.third()
    diag_z0 = Scatter(
        copies, z_plus, z_minus, z,
        lambda i: diag_sum.at[y, i, :, 0:256],
        lambda i: (diag_sum.at[y, i, 0:32, 0:256], diag_sum.at[y, i, 32:64, 0:256]),
        half_e0, full_e0,
    )
    diag_z0.first()
    diag_sum[:, z, :, 256:512] = diag_z1.third()
    diag_y1 = Scatter(
        copies, y_plus, y_minus, y,
        lambda i: diag_sum.at[i, z, :, 256:512],
        lambda i: (diag_sum.at[i, z, 0:32, 256:512], diag_sum.at[i, z, 32:64, 256:512]),
        half_e1, full_e1,
    )
    diag_y1.first()
    diag_z0.second()
    diag_y1.second()
    both = scatter_c.third()
    out_diag[...] = pivots[...] - both[0]
    out_parent[...] = (pivot_parent[...] + both[1]) * (-parent_flag)
    out_second[:, 0:256] = second_pivots[:, 0:256] + diag_z0.third()
    out_second[:, 256:512] = second_pivots[:, 256:512] + diag_y1.third()

    copies.finish()
    for at_z, copy in sigma_send:

        @pl.when(at_z != z)
        def _():
            copy.wait_send()


def per_device(sigma, panel, pivots, root_panel, parent_panel, second_pivots, first_flags, second_flags):
    vmem = pl.BlockSpec(memory_space=pltpu.VMEM)
    smem = pl.BlockSpec(memory_space=pltpu.SMEM)

    def scratch(*shape, dtype=F32):
        return pltpu.VMEM(shape, dtype)

    return pl.pallas_call(
        kernel,
        out_shape=[
            jax.ShapeDtypeStruct((256, 512), F32),
            jax.ShapeDtypeStruct((128, 512), F32),
            jax.ShapeDtypeStruct((256, 512), F32),
            jax.ShapeDtypeStruct((128, 512), F32),
            jax.ShapeDtypeStruct((64, 512), F32),
        ],
        in_specs=[smem] * 2 + [vmem] * 6,
        out_specs=[vmem] * 5,
        scratch_shapes=[
            scratch(2, 256, 256),
            scratch(4, 4, 256, 256),
            scratch(4, 256, 512),
            scratch(4, 128, 512),
            scratch(4, 4, 128, 512),
            scratch(2, 128, 512),
            scratch(4, 256, 512),
            scratch(4, 256, 512),
            scratch(2, 256, 512),
            scratch(4, 256, 512, dtype=BF16),
            scratch(4, 256, 512, dtype=BF16),
            scratch(4, 256, 512, dtype=BF16),
            scratch(4, 256, 512, dtype=BF16),
            scratch(4, 256, 512),
            scratch(2, 128, 512),
            scratch(2, 256, 512),
            scratch(4, 256, 512),
            scratch(2, 128, 512),
            scratch(2, 256, 512),
            scratch(4, 128, 256),
            scratch(4, 4, 128, 256),
            scratch(4, 2, 128, 512),
            scratch(2, 128, 512),
            scratch(2, 2, 128, 512),
            scratch(128, 512),
            scratch(4, 4, 64, 512),
            scratch(2, 2, 64, 256),
            scratch(2, 4, 64, 256),
            scratch(2, 2, 64, 256),
            scratch(2, 4, 64, 256),
            scratch(2, 32, 256),
            scratch(2, 64, 256),
            scratch(2, 32, 256),
            scratch(2, 64, 256),
            pltpu.SemaphoreType.DMA((COPIES,)),
            pltpu.SemaphoreType.DMA((COPIES,)),
            pltpu.SemaphoreType.DMA((2,)),
        ],
        compiler_params=pltpu.CompilerParams(
            collective_id=0, has_side_effects=True, vmem_limit_bytes=60 * 1024 * 1024
        ),
        cost_estimate=pl.CostEstimate(flops=13_000_000_000, bytes_accessed=4_000_000, transcendentals=0),
    )(first_flags, second_flags, sigma, panel, pivots, root_panel, parent_panel, second_pivots)


def solution(mesh):
    split_both = P("row", "col")
    return jax.shard_map(
        per_device,
        mesh=mesh,
        in_specs=(split_both,) * 6 + (P(), P()),
        out_specs=(split_both,) * 5,
        check_vma=False,
    )
```

```python
import jax
import jax.numpy as jnp
from jax import lax
from jax.experimental import pallas as pl
from jax.experimental.pallas import tpu as pltpu
from jax.sharding import PartitionSpec as P

MESH = pl.DeviceIdType.MESH
F32 = jnp.float32
BF16 = jnp.bfloat16
RING = 4
COPIES = 147
SENDS = 40
WIDE = 384


def split(value):
    high = value.astype(BF16)
    low = (value - high.astype(F32)).astype(BF16)
    return high, low


def dot3(left, right):
    (lh, ll), (rh, rl) = left, right
    total = jnp.dot(lh, rh, preferred_element_type=F32)
    total += jnp.dot(lh, rl, preferred_element_type=F32)
    total += jnp.dot(ll, rh, preferred_element_type=F32)
    return total


class Copies:
    def __init__(self, send_sems, recv_sems):
        self.send_sems, self.recv_sems = send_sems, recv_sems
        self.count = 0
        self.turn = [None] * SENDS

    def start(self, src, dst, device):
        number, place = self.count, self.count % SENDS
        self.count += 1
        if self.turn[place] is not None:
            self.turn[place].wait_send()
        copy = pltpu.make_async_remote_copy(
            src_ref=src,
            dst_ref=dst,
            send_sem=self.send_sems.at[place],
            recv_sem=self.recv_sems.at[number],
            device_id=device,
            device_id_type=MESH,
        )
        copy.start()
        self.turn[place] = copy
        return copy

    def finish(self):
        for copy in self.turn:
            if copy is not None:
                copy.wait_send()


class Gather:
    def __init__(self, copies, plus, minus, index, halves):
        self.copies, self.plus, self.minus = copies, plus, minus
        self.index, self.halves = index, halves

    def first(self):
        low, high = self.halves(self.index)
        self.plus_low = self.copies.start(low, low, self.plus)
        self.minus_high = self.copies.start(high, high, self.minus)
        self.plus_high = self.copies.start(high, high, self.plus)
        self.minus_low = self.copies.start(low, low, self.minus)

    def second(self):
        self.plus_low.wait_recv()
        half = self.halves((self.index + 3) % RING)[0]
        self.low = self.copies.start(half, half, self.plus)
        self.minus_high.wait_recv()
        half = self.halves((self.index + 1) % RING)[1]
        self.high = self.copies.start(half, half, self.minus)

    def near(self):
        self.plus_high.wait_recv()
        self.minus_low.wait_recv()

    def third(self):
        self.near()
        self.far()

    def far(self):
        self.low.wait_recv()
        self.high.wait_recv()


class Scatter:
    def __init__(self, copies, plus, minus, index, piece, halves, half_in, full_in, halves_in):
        self.copies, self.plus, self.minus = copies, plus, minus
        self.index, self.piece, self.halves = index, piece, halves
        self.half_in, self.full_in, self.halves_in = half_in, full_in, halves_in

    def first(self):
        low, high = self.halves((self.index + 2) % RING)
        self.low = self.copies.start(low, self.half_in.at[0], self.plus)
        self.high = self.copies.start(high, self.half_in.at[1], self.minus)

    def middle(self):
        high = self.halves((self.index + 1) % RING)[1]
        low = self.halves((self.index + 3) % RING)[0]
        self.early = [
            self.copies.start(high, self.halves_in(0)[1], self.plus),
            self.copies.start(low, self.halves_in(1)[0], self.minus),
        ]

    def second(self):
        self.low.wait_recv()
        half = self.halves((self.index + 1) % RING)[0]
        half[...] = half[...] + self.half_in[0]
        self.from_minus = self.copies.start(half, self.halves_in(0)[0], self.plus)
        self.high.wait_recv()
        half = self.halves((self.index + 3) % RING)[1]
        half[...] = half[...] + self.half_in[1]
        self.from_plus = self.copies.start(half, self.halves_in(1)[1], self.minus)

    def third(self):
        for copy in self.early:
            copy.wait_recv()
        self.from_minus.wait_recv()
        self.from_plus.wait_recv()
        return self.piece(self.index)[...] + self.full_in[0] + self.full_in[1]


class Direct:
    def __init__(self, copies, devices, index, piece, full_in):
        self.copies, self.devices, self.index = copies, devices, index
        self.piece, self.full_in = piece, full_in

    def first(self):
        self.sent = [
            self.copies.start(
                self.piece((self.index + step) % RING), self.full_in.at[step - 1], self.devices(step)
            )
            for step in (1, 3, 2)
        ]

    def third(self):
        for copy in self.sent:
            copy.wait_recv()
        return self.piece(self.index)[...] + self.full_in[0] + self.full_in[1] + self.full_in[2]


class Group:
    def __init__(self, copies, chip, core, index, buffer, part=None):
        self.copies, self.chip, self.core = copies, chip, core
        self.index, self.buffer, self.part = index, buffer, part

    def at(self, index):
        return self.buffer.at[index] if self.part is None else self.buffer.at[index, self.part]

    def first(self):
        own = self.at(self.index)
        self.from_chip = self.copies.start(own, own, self.chip)
        self.from_core = self.copies.start(own, own, self.core)

    def second(self):
        self.from_chip.wait_recv()
        other = self.at((self.index + 2) % RING)
        self.onward = self.copies.start(other, other, self.core)

    def third(self):
        self.from_core.wait_recv()
        self.onward.wait_recv()


def kernel(
    first_flags,
    second_flags,
    sigma,
    panel,
    pivots,
    root_panel,
    parent_panel,
    second_pivots,
    out_sigma,
    out_diag,
    out_root,
    out_parent,
    out_second,
    turned,
    blocks,
    sigma_high,
    sigma_low,
    back_high,
    back_low,
    low_group,
    pivot_group,
    parent_all,
    parent_pair,
    lower,
    lower_side,
    reduced,
    reduced_side,
    reduced_pair,
    lower_high,
    lower_low,
    red_high,
    red_low,
    side_high,
    side_low,
    red_side_high,
    red_side_low,
    sum_ay,
    half_ay,
    full_ay,
    sum_az,
    half_az,
    full_az,
    sum_by,
    half_by,
    full_by,
    sum_bz,
    half_bz,
    full_bz,
    cross_turned,
    cross_group,
    sum_f,
    half_f,
    full_f,
    sum_p,
    half_p,
    full_p,
    pivot_parent,
    diag_sum,
    half_d0,
    full_d0,
    half_d1,
    full_d1,
    full_e0,
    full_e1,
    send_sems,
    recv_sems,
    local_sems,
):
    row = lax.axis_index("row")
    col = lax.axis_index("col")
    y, z = row // RING, row % RING
    x, core = col // 2, col % 2
    local = col % RING

    def device(at_x, at_core, at_y, at_z):
        return (at_y * RING + at_z, at_x * 2 + at_core)

    def z_device(step):
        return device(x, core, y, (z + step) % RING)

    def y_device(step):
        return device(x, core, (y + step) % RING, z)

    z_plus, z_minus = z_device(1), z_device(3)
    y_plus, y_minus = y_device(1), y_device(3)
    x_plus = device((x + 1) % RING, core, y, z)
    x_minus = device((x + 3) % RING, core, y, z)
    x_pair = device(x + 1 - 2 * (x % 2), core, y, z)
    other_core = device(x, 1 - core, y, z)

    barrier = pltpu.get_barrier_semaphore()
    friends = [y_plus, y_minus, y_device(2), x_plus, x_minus]
    for step in range(RING):
        for flip in range(2):
            if step or flip:
                friends.append(device(x, (core + flip) % 2, y, (z + step) % RING))
    for friend in friends:
        pl.semaphore_signal(barrier, inc=1, device_id=friend, device_id_type=MESH)
    first_flag = first_flags[col // RING, row].astype(F32)
    root_flag = second_flags[x, row].astype(F32)
    parent_flag = second_flags[x, RING * RING + row // 2].astype(F32)
    turned[0] = sigma[:, 0:256].T
    turned[1] = sigma[:, 256:512].T
    parent_lower = parent_panel[...] * parent_flag
    parent_all[y, z] = parent_lower
    parent_pair[core] = parent_lower
    masked = panel[...] * first_flag
    low_group[local] = masked
    lower[z] = masked
    lower_side[y] = masked[:, WIDE:512]
    pl.semaphore_wait(barrier, len(friends))

    copies = Copies(send_sems, recv_sems)

    parent_y0 = Gather(
        copies, y_plus, y_minus, y,
        lambda i: (parent_all.at[i, z, 0:32], parent_all.at[i, z, 32:64]),
    )
    parent_z1 = Gather(
        copies, z_plus, z_minus, z,
        lambda i: (parent_all.at[y, i, 64:96], parent_all.at[y, i, 96:128]),
    )
    parent_z0 = Gather(
        copies, z_plus, z_minus, z,
        lambda i: (parent_all.at[0:2, i, 0:64], parent_all.at[2:4, i, 0:64]),
    )
    parent_y1 = Gather(
        copies, y_plus, y_minus, y,
        lambda i: (parent_all.at[i, 0:2, 64:128], parent_all.at[i, 2:4, 64:128]),
    )
    parent_y0.first()
    parent_z1.first()

    sigma_send = []
    for j in range(2):
        at_z = core * 2 + j
        copy = pltpu.make_async_remote_copy(
            src_ref=turned.at[j],
            dst_ref=blocks.at[x, z],
            send_sem=local_sems.at[2 + j],
            recv_sem=local_sems.at[z % 2],
            device_id=device(x, z // 2, y, at_z),
            device_id_type=MESH,
        )
        sigma_send.append((at_z, copy))

        @pl.when(at_z != z)
        def _():
            copy.start()

        @pl.when(at_z == z)
        def _():
            blocks[x, z] = turned[j]

    low_gather = Group(copies, x_pair, other_core, local, low_group)
    low_gather.first()

    def over_z(array, start, stop):
        return Gather(
            copies, z_plus, z_minus, z,
            lambda i: (array.at[i, 0:128, start:stop], array.at[i, 128:256, start:stop]),
        )

    def over_y(array):
        return Gather(
            copies, y_plus, y_minus, y,
            lambda i: (array.at[i, 0:128], array.at[i, 128:256]),
        )

    lower_z = over_z(lower, 0, WIDE)
    lower_y = over_y(lower_side)
    lower_rest = over_z(lower, WIDE, 512)
    reduced_z = over_z(reduced, 0, WIDE)
    reduced_y = over_y(reduced_side)
    reduced_rest = over_z(reduced, WIDE, 512)
    pair = parent_pair.at[core]
    pair_copy = copies.start(pair, pair, other_core)
    pivot_group[local] = pivots[...]
    parent_y0.second()
    parent_z1.second()

    for j in range(2):
        from_z = core * 2 + j

        @pl.when(from_z != z)
        def _():
            pltpu.make_async_remote_copy(
                src_ref=turned.at[j],
                dst_ref=blocks.at[x, from_z],
                send_sem=local_sems.at[2 + j],
                recv_sem=local_sems.at[j],
                device_id=other_core,
                device_id_type=MESH,
            ).wait_recv()

    sigma_gather = Gather(
        copies, x_plus, x_minus, x,
        lambda i: (blocks.at[i, 2 * core], blocks.at[i, 2 * core + 1]),
    )
    sigma_gather.first()

    def share(i):
        ref = blocks.at[i, pl.ds(2 * core, 2)]
        return copies.start(ref, ref, other_core)

    def ready(copy, i):
        copy.wait_recv()
        for k in range(RING):
            value = blocks[i, k]
            high, low = split(value)
            sigma_high[i, k] = high
            sigma_low[i, k] = low
            high, low = split(value.T)
            back_high[i, k] = high
            back_low[i, k] = low

    shared = share(x)
    parent_y0.third()
    parent_z0.first()
    parent_z1.third()
    parent_y1.first()
    lower_z.first()
    lower_y.first()
    low_gather.second()
    pivot_gather = Group(copies, x_pair, other_core, local, pivot_group)
    pivot_gather.first()
    ready(shared, x)
    parent_z0.second()
    parent_y1.second()
    lower_z.second()
    lower_y.second()
    sigma_gather.second()
    sigma_gather.near()
    shared_near = [share((x + 1) % RING), share((x + 3) % RING)]
    pivot_gather.second()
    low_gather.third()
    lower_z.third()
    lower_y.third()

    def split_rows(array, high, low, start, stop):
        for i in range(RING):
            high[i, :, start:stop], low[i, :, start:stop] = split(array[i, :, start:stop])

    split_rows(lower, lower_high, lower_low, 0, WIDE)
    split_rows(lower_side, side_high, side_low, 0, 512 - WIDE)
    ready(shared_near[0], (x + 1) % RING)
    ready(shared_near[1], (x + 3) % RING)
    parent_z0.third()
    parent_y1.third()

    total = root_panel[...] * root_flag
    for i in range(RING):
        total -= dot3(split(low_group[i]), split(parent_all[i].reshape(512, 512)))
    reduced[z] = total
    reduced_side[y] = total[:, WIDE:512]
    reduced_pair[core] = total
    reduced_z.first()
    reduced_y.first()
    ref = reduced_pair.at[core]
    reduced_copy = copies.start(ref, ref, other_core)
    sigma_gather.far()
    ready(share((x + 2) % RING), (x + 2) % RING)

    def scatter(plus, minus, index, summed, half_in, full_in, rows):
        return Scatter(
            copies, plus, minus, index,
            lambda i: summed.at[i],
            lambda i: (summed.at[i, 0 : rows // 2], summed.at[i, rows // 2 : rows]),
            half_in, full_in,
            lambda i: (full_in.at[i, 0 : rows // 2], full_in.at[i, rows // 2 : rows]),
        )

    def fill_y(into, at, high, low):
        total = None
        for i in range(RING):
            left = (sigma_high[at, i], sigma_low[at, i])
            term = dot3(left, (high[i, :, 0:WIDE], low[i, :, 0:WIDE]))
            total = term if total is None else total + term
        into[at] = total

    def fill_z(into, at, high, low):
        total = None
        for i in range(RING):
            term = dot3((back_high[i, at], back_low[i, at]), (high[i], low[i]))
            total = term if total is None else total + term
        into[at] = total

    first_y = scatter(y_plus, y_minus, y, sum_ay, half_ay, full_ay, 256)
    first_z = scatter(z_plus, z_minus, z, sum_az, half_az, full_az, 256)
    fill_y(sum_ay, (y + 2) % RING, lower_high, lower_low)
    first_y.first()
    fill_z(sum_az, (z + 2) % RING, side_high, side_low)
    first_z.first()
    for step in (1, 3):
        fill_y(sum_ay, (y + step) % RING, lower_high, lower_low)
    reduced_z.second()
    reduced_y.second()
    first_y.middle()
    first_y.second()
    for step in (1, 3):
        fill_z(sum_az, (z + step) % RING, side_high, side_low)
    first_z.middle()
    first_z.second()
    lower_rest.first()
    fill_y(sum_ay, y, lower_high, lower_low)
    fill_z(sum_az, z, side_high, side_low)
    reduced_z.third()
    split_rows(reduced, red_high, red_low, 0, WIDE)
    second_y = scatter(y_plus, y_minus, y, sum_by, half_by, full_by, 256)
    second_z = scatter(z_plus, z_minus, z, sum_bz, half_bz, full_bz, 256)
    fill_y(sum_by, (y + 2) % RING, red_high, red_low)
    cross_copies = []

    def send_cross(scattered, start, stop, output):
        cross = scattered.third() * (-first_flag)
        output[:, start:stop] = cross
        first, last = start // 128, stop // 128
        cross_turned[first:last] = cross.T.reshape(last - first, 128, 256)

    send_cross(first_y, 0, WIDE, out_sigma)
    second_y.first()
    reduced_y.third()
    split_rows(reduced_side, red_side_high, red_side_low, 0, 512 - WIDE)
    fill_z(sum_bz, (z + 2) % RING, red_side_high, red_side_low)
    send_cross(first_z, WIDE, 512, out_sigma)
    cross_group[local, z] = cross_turned[z]
    for step in (1, 3, 2):
        at_z = (z + step) % RING
        cross_copies.append(
            copies.start(cross_turned.at[at_z], cross_group.at[local, z], z_device(step))
        )
    second_z.first()
    cross_gathers = []

    def pass_on(from_z):
        gather = Group(copies, x_pair, other_core, local, cross_group, from_z)
        gather.first()
        cross_gathers.append(gather)

    pass_on(z)
    for step in (1, 3):
        fill_y(sum_by, (y + step) % RING, red_high, red_low)
    second_y.middle()
    second_y.second()
    for copy, step in zip(cross_copies, (1, 3, 2)):
        copy.wait_recv()
        pass_on((z + RING - step) % RING)
    reduced_rest.first()
    for step in (1, 3):
        fill_z(sum_bz, (z + step) % RING, red_side_high, red_side_low)
    second_z.middle()
    second_z.second()
    lower_rest.second()
    fill_y(sum_by, y, red_high, red_low)
    fill_z(sum_bz, z, red_side_high, red_side_low)

    pivot_gather.third()
    pair_copy.wait_recv()
    total = jnp.zeros((128, 512), F32)
    for i in range(RING):
        total += dot3(split(pivot_group[i]), split(parent_all[i].reshape(512, 512)))
    pivot_parent[...] = total
    right = split(total)
    for k in range(2):
        term = dot3(split(parent_pair[k].T), right)
        diag_sum[2 * k : 2 * k + 2] = term.reshape(2, RING, 64, 512)
    reduced_copy.wait_recv()
    for gather in cross_gathers:
        gather.second()
    lower_rest.third()
    split_rows(lower, lower_high, lower_low, WIDE, 512)

    for scattered, start, stop in ((second_y, 0, WIDE), (second_z, WIDE, 512)):
        result = scattered.third()
        out_root[:, start:stop] = result * (-root_flag)
        right = split(result)
        for k in range(2):
            term = dot3(split(reduced_pair[k].T), right)
            diag_sum[2 * k : 2 * k + 2, :, :, start:stop] += term.reshape(2, RING, 64, stop - start)
    diag_y0 = Scatter(
        copies, y_plus, y_minus, y,
        lambda i: diag_sum.at[i, :, :, 0:256],
        lambda i: (diag_sum.at[i, 0:2, :, 0:256], diag_sum.at[i, 2:4, :, 0:256]),
        half_d0, full_d0,
        lambda i: (full_d0.at[i, 0:2], full_d0.at[i, 2:4]),
    )
    diag_z1 = Scatter(
        copies, z_plus, z_minus, z,
        lambda i: diag_sum.at[:, i, :, 256:512],
        lambda i: (diag_sum.at[0:2, i, :, 256:512], diag_sum.at[2:4, i, :, 256:512]),
        half_d1, full_d1,
        lambda i: (full_d1.at[i, 0:2], full_d1.at[i, 2:4]),
    )
    diag_y0.first()
    diag_z1.first()
    diag_y0.middle()
    diag_z1.middle()
    reduced_rest.second()
    for gather in cross_gathers:
        gather.third()

    def node_fill(into, at, high, low):
        total = None
        for i in range(RING):
            term = dot3(split(cross_group[at, i]), (high[i], low[i]))
            total = term if total is None else total + term
        into[at] = total

    node_f = scatter(y_plus, y_minus, y, sum_f, half_f, full_f, 128)
    node_p = scatter(y_plus, y_minus, y, sum_p, half_p, full_p, 128)
    node_fill(sum_f, (y + 2) % RING, lower_high, lower_low)
    node_f.first()
    diag_y0.second()
    diag_z1.second()
    for step in (1, 3):
        node_fill(sum_f, (y + step) % RING, lower_high, lower_low)
    node_f.middle()
    node_f.second()
    reduced_rest.third()
    split_rows(reduced, red_high, red_low, WIDE, 512)
    node_fill(sum_p, (y + 2) % RING, red_high, red_low)
    node_p.first()
    diag_sum[y, :, :, 0:256] = diag_y0.third()
    diag_z0 = Direct(copies, z_device, z, lambda i: diag_sum.at[y, i, :, 0:256], full_e0)
    diag_z0.first()
    diag_sum[:, z, :, 256:512] = diag_z1.third()
    diag_y1 = Direct(copies, y_device, y, lambda i: diag_sum.at[i, z, :, 256:512], full_e1)
    diag_y1.first()
    for step in (1, 3):
        node_fill(sum_p, (y + step) % RING, red_high, red_low)
    node_p.middle()
    node_p.second()
    node_fill(sum_f, y, lower_high, lower_low)
    node_fill(sum_p, y, red_high, red_low)
    out_diag[...] = pivots[...] - node_f.third()
    out_second[:, 0:256] = second_pivots[:, 0:256] + diag_z0.third()
    out_second[:, 256:512] = second_pivots[:, 256:512] + diag_y1.third()
    out_parent[...] = (pivot_parent[...] + node_p.third()) * (-parent_flag)

    copies.finish()
    for at_z, copy in sigma_send:

        @pl.when(at_z != z)
        def _():
            copy.wait_send()


def hand_over(*refs):
    for result, output in zip(refs[:5], refs[5:]):
        output[...] = result[...]


def per_device(sigma, panel, pivots, root_panel, parent_panel, second_pivots, first_flags, second_flags):
    vmem = pl.BlockSpec(memory_space=pltpu.VMEM)
    smem = pl.BlockSpec(memory_space=pltpu.SMEM)

    def scratch(*shape, dtype=F32):
        return pltpu.VMEM(shape, dtype)

    results = pl.pallas_call(
        kernel,
        out_shape=[
            jax.ShapeDtypeStruct((256, 512), F32),
            jax.ShapeDtypeStruct((128, 512), F32),
            jax.ShapeDtypeStruct((256, 512), F32),
            jax.ShapeDtypeStruct((128, 512), F32),
            jax.ShapeDtypeStruct((64, 512), F32),
        ],
        in_specs=[smem] * 2 + [vmem] * 6,
        out_specs=[vmem] * 5,
        scratch_shapes=[
            scratch(2, 256, 256),
            scratch(4, 4, 256, 256),
            scratch(4, 4, 256, 256, dtype=BF16),
            scratch(4, 4, 256, 256, dtype=BF16),
            scratch(4, 4, 256, 256, dtype=BF16),
            scratch(4, 4, 256, 256, dtype=BF16),
            scratch(4, 256, 512),
            scratch(4, 128, 512),
            scratch(4, 4, 128, 512),
            scratch(2, 128, 512),
            scratch(4, 256, 512),
            scratch(4, 256, 512 - WIDE),
            scratch(4, 256, 512),
            scratch(4, 256, 512 - WIDE),
            scratch(2, 256, 512),
            scratch(4, 256, 512, dtype=BF16),
            scratch(4, 256, 512, dtype=BF16),
            scratch(4, 256, 512, dtype=BF16),
            scratch(4, 256, 512, dtype=BF16),
            scratch(4, 256, 512 - WIDE, dtype=BF16),
            scratch(4, 256, 512 - WIDE, dtype=BF16),
            scratch(4, 256, 512 - WIDE, dtype=BF16),
            scratch(4, 256, 512 - WIDE, dtype=BF16),
            scratch(4, 256, WIDE),
            scratch(2, 128, WIDE),
            scratch(2, 256, WIDE),
            scratch(4, 256, 512 - WIDE),
            scratch(2, 128, 512 - WIDE),
            scratch(2, 256, 512 - WIDE),
            scratch(4, 256, WIDE),
            scratch(2, 128, WIDE),
            scratch(2, 256, WIDE),
            scratch(4, 256, 512 - WIDE),
            scratch(2, 128, 512 - WIDE),
            scratch(2, 256, 512 - WIDE),
            scratch(4, 128, 256),
            scratch(4, 4, 128, 256),
            scratch(4, 128, 512),
            scratch(2, 64, 512),
            scratch(2, 128, 512),
            scratch(4, 128, 512),
            scratch(2, 64, 512),
            scratch(2, 128, 512),
            scratch(128, 512),
            scratch(4, 4, 64, 512),
            scratch(2, 2, 64, 256),
            scratch(2, 4, 64, 256),
            scratch(2, 2, 64, 256),
            scratch(2, 4, 64, 256),
            scratch(3, 64, 256),
            scratch(3, 64, 256),
            pltpu.SemaphoreType.DMA((SENDS,)),
            pltpu.SemaphoreType.DMA((COPIES,)),
            pltpu.SemaphoreType.DMA((4,)),
        ],
        compiler_params=pltpu.CompilerParams(
            collective_id=0, has_side_effects=True, vmem_limit_bytes=60 * 1024 * 1024
        ),
        cost_estimate=pl.CostEstimate(flops=13_000_000_000, bytes_accessed=4_000_000, transcendentals=0),
    )(first_flags, second_flags, sigma, panel, pivots, root_panel, parent_panel, second_pivots)
    return pl.pallas_call(
        hand_over,
        out_shape=[jax.ShapeDtypeStruct(r.shape, r.dtype) for r in results],
        in_specs=[vmem] * 5,
        out_specs=[vmem] * 5,
    )(*results)


def solution(mesh):
    split_both = P("row", "col")
    return jax.shard_map(
        per_device,
        mesh=mesh,
        in_specs=(split_both,) * 6 + (P(), P()),
        out_specs=(split_both,) * 5,
        check_vma=False,
    )
```

```python
import jax
import jax.numpy as jnp
from jax import lax
from jax.experimental import pallas as pl
from jax.experimental.pallas import tpu as pltpu
from jax.sharding import PartitionSpec as P

MESH = pl.DeviceIdType.MESH
F32 = jnp.float32
BF16 = jnp.bfloat16
RING = 4
COPIES = 147
SENDS = 40
WIDE = 384


def split(value):
    high = value.astype(BF16)
    low = (value - high.astype(F32)).astype(BF16)
    return high, low


def dot3(left, right):
    (lh, ll), (rh, rl) = left, right
    total = jnp.dot(lh, rh, preferred_element_type=F32)
    total += jnp.dot(lh, rl, preferred_element_type=F32)
    total += jnp.dot(ll, rh, preferred_element_type=F32)
    return total


class Copies:
    def __init__(self, send_sems, recv_sems):
        self.send_sems, self.recv_sems = send_sems, recv_sems
        self.count = 0
        self.turn = [None] * SENDS

    def start(self, src, dst, device):
        number, place = self.count, self.count % SENDS
        self.count += 1
        if self.turn[place] is not None:
            self.turn[place].wait_send()
        copy = pltpu.make_async_remote_copy(
            src_ref=src,
            dst_ref=dst,
            send_sem=self.send_sems.at[place],
            recv_sem=self.recv_sems.at[number],
            device_id=device,
            device_id_type=MESH,
        )
        copy.start()
        self.turn[place] = copy
        return copy

    def finish(self):
        for copy in self.turn:
            if copy is not None:
                copy.wait_send()


class Gather:
    def __init__(self, copies, plus, minus, index, halves):
        self.copies, self.plus, self.minus = copies, plus, minus
        self.index, self.halves = index, halves

    def first(self):
        low, high = self.halves(self.index)
        self.plus_low = self.copies.start(low, low, self.plus)
        self.minus_high = self.copies.start(high, high, self.minus)
        self.plus_high = self.copies.start(high, high, self.plus)
        self.minus_low = self.copies.start(low, low, self.minus)

    def second(self):
        self.plus_low.wait_recv()
        half = self.halves((self.index + 3) % RING)[0]
        self.low = self.copies.start(half, half, self.plus)
        self.minus_high.wait_recv()
        half = self.halves((self.index + 1) % RING)[1]
        self.high = self.copies.start(half, half, self.minus)

    def near(self):
        self.plus_high.wait_recv()
        self.minus_low.wait_recv()

    def third(self):
        self.near()
        self.far()

    def far(self):
        self.low.wait_recv()
        self.high.wait_recv()


class Scatter:
    def __init__(self, copies, plus, minus, index, piece, halves, half_in, full_in, halves_in):
        self.copies, self.plus, self.minus = copies, plus, minus
        self.index, self.piece, self.halves = index, piece, halves
        self.half_in, self.full_in, self.halves_in = half_in, full_in, halves_in

    def first(self):
        low, high = self.halves((self.index + 2) % RING)
        self.low = self.copies.start(low, self.half_in.at[0], self.plus)
        self.high = self.copies.start(high, self.half_in.at[1], self.minus)

    def middle(self):
        high = self.halves((self.index + 1) % RING)[1]
        low = self.halves((self.index + 3) % RING)[0]
        self.early = [
            self.copies.start(high, self.halves_in(0)[1], self.plus),
            self.copies.start(low, self.halves_in(1)[0], self.minus),
        ]

    def second(self):
        self.low.wait_recv()
        half = self.halves((self.index + 1) % RING)[0]
        half[...] = half[...] + self.half_in[0]
        self.from_minus = self.copies.start(half, self.halves_in(0)[0], self.plus)
        self.high.wait_recv()
        half = self.halves((self.index + 3) % RING)[1]
        half[...] = half[...] + self.half_in[1]
        self.from_plus = self.copies.start(half, self.halves_in(1)[1], self.minus)

    def third(self):
        for copy in self.early:
            copy.wait_recv()
        self.from_minus.wait_recv()
        self.from_plus.wait_recv()
        return self.piece(self.index)[...] + self.full_in[0] + self.full_in[1]


class Direct:
    def __init__(self, copies, devices, index, piece, full_in):
        self.copies, self.devices, self.index = copies, devices, index
        self.piece, self.full_in = piece, full_in

    def first(self):
        self.sent = [
            self.copies.start(
                self.piece((self.index + step) % RING), self.full_in.at[step - 1], self.devices(step)
            )
            for step in (1, 3, 2)
        ]

    def third(self):
        for copy in self.sent:
            copy.wait_recv()
        return self.piece(self.index)[...] + self.full_in[0] + self.full_in[1] + self.full_in[2]


class Group:
    def __init__(self, copies, chip, core, index, buffer, part=None):
        self.copies, self.chip, self.core = copies, chip, core
        self.index, self.buffer, self.part = index, buffer, part

    def at(self, index):
        return self.buffer.at[index] if self.part is None else self.buffer.at[index, self.part]

    def first(self):
        own = self.at(self.index)
        self.from_chip = self.copies.start(own, own, self.chip)
        self.from_core = self.copies.start(own, own, self.core)

    def second(self):
        self.from_chip.wait_recv()
        other = self.at((self.index + 2) % RING)
        self.onward = self.copies.start(other, other, self.core)

    def third(self):
        self.from_core.wait_recv()
        self.onward.wait_recv()


def kernel(
    first_flags,
    second_flags,
    sigma,
    panel,
    pivots,
    root_panel,
    parent_panel,
    second_pivots,
    out_sigma,
    out_diag,
    out_root,
    out_parent,
    out_second,
    turned,
    blocks,
    sigma_high,
    sigma_low,
    back_high,
    back_low,
    low_group,
    pivot_group,
    parent_all,
    parent_pair,
    lower,
    lower_side,
    reduced,
    reduced_side,
    reduced_pair,
    lower_high,
    lower_low,
    red_high,
    red_low,
    side_high,
    side_low,
    red_side_high,
    red_side_low,
    sum_ay,
    half_ay,
    full_ay,
    sum_az,
    half_az,
    full_az,
    sum_by,
    half_by,
    full_by,
    sum_bz,
    half_bz,
    full_bz,
    cross_turned,
    cross_group,
    sum_f,
    half_f,
    full_f,
    sum_p,
    half_p,
    full_p,
    pivot_parent,
    diag_sum,
    half_d0,
    full_d0,
    half_d1,
    full_d1,
    full_e0,
    full_e1,
    send_sems,
    recv_sems,
    local_sems,
):
    row = lax.axis_index("row")
    col = lax.axis_index("col")
    y, z = row // RING, row % RING
    x, core = col // 2, col % 2
    local = col % RING

    def device(at_x, at_core, at_y, at_z):
        return (at_y * RING + at_z, at_x * 2 + at_core)

    def z_device(step):
        return device(x, core, y, (z + step) % RING)

    def y_device(step):
        return device(x, core, (y + step) % RING, z)

    z_plus, z_minus = z_device(1), z_device(3)
    y_plus, y_minus = y_device(1), y_device(3)
    x_plus = device((x + 1) % RING, core, y, z)
    x_minus = device((x + 3) % RING, core, y, z)
    x_pair = device(x + 1 - 2 * (x % 2), core, y, z)
    other_core = device(x, 1 - core, y, z)

    barrier = pltpu.get_barrier_semaphore()
    friends = [y_plus, y_minus, y_device(2), x_plus, x_minus]
    for step in range(RING):
        for flip in range(2):
            if step or flip:
                friends.append(device(x, (core + flip) % 2, y, (z + step) % RING))
    for friend in friends:
        pl.semaphore_signal(barrier, inc=1, device_id=friend, device_id_type=MESH)
    first_flag = first_flags[col // RING, row].astype(F32)
    root_flag = second_flags[x, row].astype(F32)
    parent_flag = second_flags[x, RING * RING + row // 2].astype(F32)
    turned[0] = sigma[:, 0:256].T
    turned[1] = sigma[:, 256:512].T
    parent_lower = parent_panel[...] * parent_flag
    parent_all[y, z] = parent_lower
    parent_pair[core] = parent_lower
    masked = panel[...] * first_flag
    low_group[local] = masked
    lower[z] = masked
    lower_side[y] = masked[:, WIDE:512]
    pl.semaphore_wait(barrier, len(friends))

    copies = Copies(send_sems, recv_sems)

    parent_y0 = Gather(
        copies, y_plus, y_minus, y,
        lambda i: (parent_all.at[i, z, 0:24], parent_all.at[i, z, 24:48]),
    )
    parent_z1 = Gather(
        copies, z_plus, z_minus, z,
        lambda i: (parent_all.at[y, i, 48:88], parent_all.at[y, i, 88:128]),
    )
    parent_z0 = Gather(
        copies, z_plus, z_minus, z,
        lambda i: (parent_all.at[0:2, i, 0:48], parent_all.at[2:4, i, 0:48]),
    )
    parent_y1 = Gather(
        copies, y_plus, y_minus, y,
        lambda i: (parent_all.at[i, 0:2, 48:128], parent_all.at[i, 2:4, 48:128]),
    )
    parent_y0.first()
    parent_z1.first()

    sigma_send = []
    for j in range(2):
        at_z = core * 2 + j
        copy = pltpu.make_async_remote_copy(
            src_ref=turned.at[j],
            dst_ref=blocks.at[x, z],
            send_sem=local_sems.at[2 + j],
            recv_sem=local_sems.at[z % 2],
            device_id=device(x, z // 2, y, at_z),
            device_id_type=MESH,
        )
        sigma_send.append((at_z, copy))

        @pl.when(at_z != z)
        def _():
            copy.start()

        @pl.when(at_z == z)
        def _():
            blocks[x, z] = turned[j]

    low_gather = Group(copies, x_pair, other_core, local, low_group)
    low_gather.first()

    def over_z(array, start, stop):
        return Gather(
            copies, z_plus, z_minus, z,
            lambda i: (array.at[i, 0:128, start:stop], array.at[i, 128:256, start:stop]),
        )

    def over_y(array):
        return Gather(
            copies, y_plus, y_minus, y,
            lambda i: (array.at[i, 0:128], array.at[i, 128:256]),
        )

    lower_z = over_z(lower, 0, WIDE)
    lower_y = over_y(lower_side)
    lower_rest = over_z(lower, WIDE, 512)
    reduced_z = over_z(reduced, 0, WIDE)
    reduced_y = over_y(reduced_side)
    reduced_rest = over_z(reduced, WIDE, 512)
    pair = parent_pair.at[core]
    pair_copy = copies.start(pair, pair, other_core)
    pivot_group[local] = pivots[...]
    parent_y0.second()
    parent_z1.second()

    for j in range(2):
        from_z = core * 2 + j

        @pl.when(from_z != z)
        def _():
            pltpu.make_async_remote_copy(
                src_ref=turned.at[j],
                dst_ref=blocks.at[x, from_z],
                send_sem=local_sems.at[2 + j],
                recv_sem=local_sems.at[j],
                device_id=other_core,
                device_id_type=MESH,
            ).wait_recv()

    sigma_gather = Gather(
        copies, x_plus, x_minus, x,
        lambda i: (blocks.at[i, 2 * core], blocks.at[i, 2 * core + 1]),
    )
    sigma_gather.first()

    def share(i):
        ref = blocks.at[i, pl.ds(2 * core, 2)]
        return copies.start(ref, ref, other_core)

    def ready(copy, i):
        copy.wait_recv()
        for k in range(RING):
            value = blocks[i, k]
            high, low = split(value)
            sigma_high[i, k] = high
            sigma_low[i, k] = low
            high, low = split(value.T)
            back_high[i, k] = high
            back_low[i, k] = low

    shared = share(x)
    parent_y0.third()
    parent_z0.first()
    parent_z1.third()
    parent_y1.first()
    lower_z.first()
    lower_y.first()
    low_gather.second()
    pivot_gather = Group(copies, x_pair, other_core, local, pivot_group)
    pivot_gather.first()
    ready(shared, x)
    parent_z0.second()
    parent_y1.second()
    lower_z.second()
    lower_y.second()
    sigma_gather.second()
    sigma_gather.near()
    shared_near = [share((x + 1) % RING), share((x + 3) % RING)]
    pivot_gather.second()
    low_gather.third()
    lower_z.third()
    lower_y.third()

    def split_rows(array, high, low, start, stop):
        for i in range(RING):
            high[i, :, start:stop], low[i, :, start:stop] = split(array[i, :, start:stop])

    split_rows(lower, lower_high, lower_low, 0, WIDE)
    split_rows(lower_side, side_high, side_low, 0, 512 - WIDE)
    ready(shared_near[0], (x + 1) % RING)
    ready(shared_near[1], (x + 3) % RING)
    parent_z0.third()
    parent_y1.third()

    total = root_panel[...] * root_flag
    for i in range(RING):
        total -= dot3(split(low_group[i]), split(parent_all[i].reshape(512, 512)))
    reduced[z] = total
    reduced_side[y] = total[:, WIDE:512]
    reduced_pair[core] = total
    reduced_z.first()
    reduced_y.first()
    ref = reduced_pair.at[core]
    reduced_copy = copies.start(ref, ref, other_core)
    sigma_gather.far()
    ready(share((x + 2) % RING), (x + 2) % RING)

    def scatter(plus, minus, index, summed, half_in, full_in, rows):
        return Scatter(
            copies, plus, minus, index,
            lambda i: summed.at[i],
            lambda i: (summed.at[i, 0 : rows // 2], summed.at[i, rows // 2 : rows]),
            half_in, full_in,
            lambda i: (full_in.at[i, 0 : rows // 2], full_in.at[i, rows // 2 : rows]),
        )

    def fill_y(into, at, high, low):
        total = None
        for i in range(RING):
            left = (sigma_high[at, i], sigma_low[at, i])
            term = dot3(left, (high[i, :, 0:WIDE], low[i, :, 0:WIDE]))
            total = term if total is None else total + term
        into[at] = total

    def fill_z(into, at, high, low):
        total = None
        for i in range(RING):
            term = dot3((back_high[i, at], back_low[i, at]), (high[i], low[i]))
            total = term if total is None else total + term
        into[at] = total

    first_y = scatter(y_plus, y_minus, y, sum_ay, half_ay, full_ay, 256)
    first_z = scatter(z_plus, z_minus, z, sum_az, half_az, full_az, 256)
    fill_y(sum_ay, (y + 2) % RING, lower_high, lower_low)
    first_y.first()
    fill_z(sum_az, (z + 2) % RING, side_high, side_low)
    first_z.first()
    reduced_z.second()
    reduced_y.second()
    for step in (1, 3):
        fill_y(sum_ay, (y + step) % RING, lower_high, lower_low)
    first_y.middle()
    first_y.second()
    for step in (1, 3):
        fill_z(sum_az, (z + step) % RING, side_high, side_low)
    first_z.middle()
    first_z.second()
    lower_rest.first()
    fill_y(sum_ay, y, lower_high, lower_low)
    fill_z(sum_az, z, side_high, side_low)
    reduced_z.third()
    split_rows(reduced, red_high, red_low, 0, WIDE)
    second_y = scatter(y_plus, y_minus, y, sum_by, half_by, full_by, 256)
    second_z = scatter(z_plus, z_minus, z, sum_bz, half_bz, full_bz, 256)
    fill_y(sum_by, (y + 2) % RING, red_high, red_low)
    cross_copies = []

    def send_cross(scattered, start, stop, output):
        cross = scattered.third() * (-first_flag)
        output[:, start:stop] = cross
        first, last = start // 128, stop // 128
        cross_turned[first:last] = cross.T.reshape(last - first, 128, 256)

    send_cross(first_y, 0, WIDE, out_sigma)
    second_y.first()
    reduced_y.third()
    split_rows(reduced_side, red_side_high, red_side_low, 0, 512 - WIDE)
    fill_z(sum_bz, (z + 2) % RING, red_side_high, red_side_low)
    send_cross(first_z, WIDE, 512, out_sigma)
    cross_group[local, z] = cross_turned[z]
    for step in (1, 3, 2):
        at_z = (z + step) % RING
        cross_copies.append(
            copies.start(cross_turned.at[at_z], cross_group.at[local, z], z_device(step))
        )
    second_z.first()
    cross_gathers = []

    def pass_on(from_z):
        gather = Group(copies, x_pair, other_core, local, cross_group, from_z)
        gather.first()
        cross_gathers.append(gather)

    pass_on(z)
    for step in (1, 3):
        fill_y(sum_by, (y + step) % RING, red_high, red_low)
    second_y.middle()
    second_y.second()
    for copy, step in zip(cross_copies, (1, 3, 2)):
        copy.wait_recv()
        pass_on((z + RING - step) % RING)
    reduced_rest.first()
    for step in (1, 3):
        fill_z(sum_bz, (z + step) % RING, red_side_high, red_side_low)
    second_z.middle()
    second_z.second()
    lower_rest.second()
    fill_y(sum_by, y, red_high, red_low)
    fill_z(sum_bz, z, red_side_high, red_side_low)

    pivot_gather.third()
    pair_copy.wait_recv()
    total = jnp.zeros((128, 512), F32)
    for i in range(RING):
        total += dot3(split(pivot_group[i]), split(parent_all[i].reshape(512, 512)))
    pivot_parent[...] = total
    right = split(total)
    for k in range(2):
        term = dot3(split(parent_pair[k].T), right)
        diag_sum[2 * k : 2 * k + 2] = term.reshape(2, RING, 64, 512)
    reduced_copy.wait_recv()
    for gather in cross_gathers:
        gather.second()
    lower_rest.third()
    split_rows(lower, lower_high, lower_low, WIDE, 512)

    for scattered, start, stop in ((second_y, 0, WIDE), (second_z, WIDE, 512)):
        result = scattered.third()
        out_root[:, start:stop] = result * (-root_flag)
        right = split(result)
        for k in range(2):
            term = dot3(split(reduced_pair[k].T), right)
            diag_sum[2 * k : 2 * k + 2, :, :, start:stop] += term.reshape(2, RING, 64, stop - start)
    diag_y0 = Scatter(
        copies, y_plus, y_minus, y,
        lambda i: diag_sum.at[i, :, :, 0:128],
        lambda i: (diag_sum.at[i, 0:2, :, 0:128], diag_sum.at[i, 2:4, :, 0:128]),
        half_d0, full_d0,
        lambda i: (full_d0.at[i, 0:2], full_d0.at[i, 2:4]),
    )
    diag_z1 = Scatter(
        copies, z_plus, z_minus, z,
        lambda i: diag_sum.at[:, i, :, 128:512],
        lambda i: (diag_sum.at[0:2, i, :, 128:512], diag_sum.at[2:4, i, :, 128:512]),
        half_d1, full_d1,
        lambda i: (full_d1.at[i, 0:2], full_d1.at[i, 2:4]),
    )
    diag_y0.first()
    diag_z1.first()
    diag_y0.middle()
    diag_z1.middle()
    reduced_rest.second()
    for gather in cross_gathers:
        gather.third()

    def node_fill(into, at, high, low):
        total = None
        for i in range(RING):
            term = dot3(split(cross_group[at, i]), (high[i], low[i]))
            total = term if total is None else total + term
        into[at] = total

    node_f = scatter(y_plus, y_minus, y, sum_f, half_f, full_f, 128)
    node_p = scatter(y_plus, y_minus, y, sum_p, half_p, full_p, 128)
    node_fill(sum_f, (y + 2) % RING, lower_high, lower_low)
    node_f.first()
    diag_y0.second()
    diag_z1.second()
    for step in (1, 3):
        node_fill(sum_f, (y + step) % RING, lower_high, lower_low)
    node_f.middle()
    node_f.second()
    reduced_rest.third()
    split_rows(reduced, red_high, red_low, WIDE, 512)
    node_fill(sum_p, (y + 2) % RING, red_high, red_low)
    node_p.first()
    diag_sum[y, :, :, 0:128] = diag_y0.third()
    diag_z0 = Direct(copies, z_device, z, lambda i: diag_sum.at[y, i, :, 0:128], full_e0)
    diag_z0.first()
    diag_sum[:, z, :, 128:512] = diag_z1.third()
    diag_y1 = Direct(copies, y_device, y, lambda i: diag_sum.at[i, z, :, 128:512], full_e1)
    diag_y1.first()
    for step in (1, 3):
        node_fill(sum_p, (y + step) % RING, red_high, red_low)
    node_p.middle()
    node_p.second()
    node_fill(sum_f, y, lower_high, lower_low)
    node_fill(sum_p, y, red_high, red_low)
    out_diag[...] = pivots[...] - node_f.third()
    out_second[:, 0:128] = second_pivots[:, 0:128] + diag_z0.third()
    out_second[:, 128:512] = second_pivots[:, 128:512] + diag_y1.third()
    out_parent[...] = (pivot_parent[...] + node_p.third()) * (-parent_flag)

    copies.finish()
    for at_z, copy in sigma_send:

        @pl.when(at_z != z)
        def _():
            copy.wait_send()


def hand_over(*refs):
    for result, output in zip(refs[:5], refs[5:]):
        output[...] = result[...]


def per_device(sigma, panel, pivots, root_panel, parent_panel, second_pivots, first_flags, second_flags):
    vmem = pl.BlockSpec(memory_space=pltpu.VMEM)
    smem = pl.BlockSpec(memory_space=pltpu.SMEM)

    def scratch(*shape, dtype=F32):
        return pltpu.VMEM(shape, dtype)

    results = pl.pallas_call(
        kernel,
        out_shape=[
            jax.ShapeDtypeStruct((256, 512), F32),
            jax.ShapeDtypeStruct((128, 512), F32),
            jax.ShapeDtypeStruct((256, 512), F32),
            jax.ShapeDtypeStruct((128, 512), F32),
            jax.ShapeDtypeStruct((64, 512), F32),
        ],
        in_specs=[smem] * 2 + [vmem] * 6,
        out_specs=[vmem] * 5,
        scratch_shapes=[
            scratch(2, 256, 256),
            scratch(4, 4, 256, 256),
            scratch(4, 4, 256, 256, dtype=BF16),
            scratch(4, 4, 256, 256, dtype=BF16),
            scratch(4, 4, 256, 256, dtype=BF16),
            scratch(4, 4, 256, 256, dtype=BF16),
            scratch(4, 256, 512),
            scratch(4, 128, 512),
            scratch(4, 4, 128, 512),
            scratch(2, 128, 512),
            scratch(4, 256, 512),
            scratch(4, 256, 512 - WIDE),
            scratch(4, 256, 512),
            scratch(4, 256, 512 - WIDE),
            scratch(2, 256, 512),
            scratch(4, 256, 512, dtype=BF16),
            scratch(4, 256, 512, dtype=BF16),
            scratch(4, 256, 512, dtype=BF16),
            scratch(4, 256, 512, dtype=BF16),
            scratch(4, 256, 512 - WIDE, dtype=BF16),
            scratch(4, 256, 512 - WIDE, dtype=BF16),
            scratch(4, 256, 512 - WIDE, dtype=BF16),
            scratch(4, 256, 512 - WIDE, dtype=BF16),
            scratch(4, 256, WIDE),
            scratch(2, 128, WIDE),
            scratch(2, 256, WIDE),
            scratch(4, 256, 512 - WIDE),
            scratch(2, 128, 512 - WIDE),
            scratch(2, 256, 512 - WIDE),
            scratch(4, 256, WIDE),
            scratch(2, 128, WIDE),
            scratch(2, 256, WIDE),
            scratch(4, 256, 512 - WIDE),
            scratch(2, 128, 512 - WIDE),
            scratch(2, 256, 512 - WIDE),
            scratch(4, 128, 256),
            scratch(4, 4, 128, 256),
            scratch(4, 128, 512),
            scratch(2, 64, 512),
            scratch(2, 128, 512),
            scratch(4, 128, 512),
            scratch(2, 64, 512),
            scratch(2, 128, 512),
            scratch(128, 512),
            scratch(4, 4, 64, 512),
            scratch(2, 2, 64, 128),
            scratch(2, 4, 64, 128),
            scratch(2, 2, 64, 384),
            scratch(2, 4, 64, 384),
            scratch(3, 64, 128),
            scratch(3, 64, 384),
            pltpu.SemaphoreType.DMA((SENDS,)),
            pltpu.SemaphoreType.DMA((COPIES,)),
            pltpu.SemaphoreType.DMA((4,)),
        ],
        compiler_params=pltpu.CompilerParams(
            collective_id=0, has_side_effects=True, vmem_limit_bytes=60 * 1024 * 1024
        ),
        cost_estimate=pl.CostEstimate(flops=13_000_000_000, bytes_accessed=4_000_000, transcendentals=0),
    )(first_flags, second_flags, sigma, panel, pivots, root_panel, parent_panel, second_pivots)
    return pl.pallas_call(
        hand_over,
        out_shape=[jax.ShapeDtypeStruct(r.shape, r.dtype) for r in results],
        in_specs=[vmem] * 5,
        out_specs=[vmem] * 5,
    )(*results)


def solution(mesh):
    split_both = P("row", "col")
    return jax.shard_map(
        per_device,
        mesh=mesh,
        in_specs=(split_both,) * 6 + (P(), P()),
        out_specs=(split_both,) * 5,
        check_vma=False,
    )
```

```python
import jax
import jax.numpy as jnp
from jax import lax
from jax.experimental import pallas as pl
from jax.experimental.pallas import tpu as pltpu
from jax.sharding import PartitionSpec as P

MESH = pl.DeviceIdType.MESH
F32 = jnp.float32
BF16 = jnp.bfloat16
RING = 4
COPIES = 147
SENDS = 40
WIDE = 384


def split(value):
    high = value.astype(BF16)
    low = (value - high.astype(F32)).astype(BF16)
    return high, low


def dot3(left, right):
    (lh, ll), (rh, rl) = left, right
    total = jnp.dot(lh, rh, preferred_element_type=F32)
    total += jnp.dot(lh, rl, preferred_element_type=F32)
    total += jnp.dot(ll, rh, preferred_element_type=F32)
    return total


class Copies:
    def __init__(self, send_sems, recv_sems):
        self.send_sems, self.recv_sems = send_sems, recv_sems
        self.count = 0
        self.turn = [None] * SENDS

    def start(self, src, dst, device):
        number, place = self.count, self.count % SENDS
        self.count += 1
        if self.turn[place] is not None:
            self.turn[place].wait_send()
        copy = pltpu.make_async_remote_copy(
            src_ref=src,
            dst_ref=dst,
            send_sem=self.send_sems.at[place],
            recv_sem=self.recv_sems.at[number],
            device_id=device,
            device_id_type=MESH,
        )
        copy.start()
        self.turn[place] = copy
        return copy

    def finish(self):
        for copy in self.turn:
            if copy is not None:
                copy.wait_send()


class Gather:
    def __init__(self, copies, plus, minus, index, halves):
        self.copies, self.plus, self.minus = copies, plus, minus
        self.index, self.halves = index, halves

    def first(self):
        low, high = self.halves(self.index)
        self.plus_low = self.copies.start(low, low, self.plus)
        self.minus_high = self.copies.start(high, high, self.minus)
        self.plus_high = self.copies.start(high, high, self.plus)
        self.minus_low = self.copies.start(low, low, self.minus)

    def second(self):
        self.plus_low.wait_recv()
        half = self.halves((self.index + 3) % RING)[0]
        self.low = self.copies.start(half, half, self.plus)
        self.minus_high.wait_recv()
        half = self.halves((self.index + 1) % RING)[1]
        self.high = self.copies.start(half, half, self.minus)

    def near(self):
        self.plus_high.wait_recv()
        self.minus_low.wait_recv()

    def third(self):
        self.near()
        self.far()

    def far(self):
        self.low.wait_recv()
        self.high.wait_recv()


class Scatter:
    def __init__(self, copies, plus, minus, index, piece, halves, half_in, full_in, halves_in):
        self.copies, self.plus, self.minus = copies, plus, minus
        self.index, self.piece, self.halves = index, piece, halves
        self.half_in, self.full_in, self.halves_in = half_in, full_in, halves_in

    def first(self):
        low, high = self.halves((self.index + 2) % RING)
        self.low = self.copies.start(low, self.half_in.at[0], self.plus)
        self.high = self.copies.start(high, self.half_in.at[1], self.minus)

    def middle(self):
        high = self.halves((self.index + 1) % RING)[1]
        low = self.halves((self.index + 3) % RING)[0]
        self.early = [
            self.copies.start(high, self.halves_in(0)[1], self.plus),
            self.copies.start(low, self.halves_in(1)[0], self.minus),
        ]

    def second(self):
        self.low.wait_recv()
        half = self.halves((self.index + 1) % RING)[0]
        half[...] = half[...] + self.half_in[0]
        self.from_minus = self.copies.start(half, self.halves_in(0)[0], self.plus)
        self.high.wait_recv()
        half = self.halves((self.index + 3) % RING)[1]
        half[...] = half[...] + self.half_in[1]
        self.from_plus = self.copies.start(half, self.halves_in(1)[1], self.minus)

    def third(self):
        for copy in self.early:
            copy.wait_recv()
        self.from_minus.wait_recv()
        self.from_plus.wait_recv()
        return self.piece(self.index)[...] + self.full_in[0] + self.full_in[1]


class Direct:
    def __init__(self, copies, devices, index, piece, full_in):
        self.copies, self.devices, self.index = copies, devices, index
        self.piece, self.full_in = piece, full_in

    def first(self):
        self.sent = [
            self.copies.start(
                self.piece((self.index + step) % RING), self.full_in.at[step - 1], self.devices(step)
            )
            for step in (1, 3, 2)
        ]

    def third(self):
        for copy in self.sent:
            copy.wait_recv()
        return self.piece(self.index)[...] + self.full_in[0] + self.full_in[1] + self.full_in[2]


class Group:
    def __init__(self, copies, chip, core, index, buffer, part=None):
        self.copies, self.chip, self.core = copies, chip, core
        self.index, self.buffer, self.part = index, buffer, part

    def at(self, index):
        return self.buffer.at[index] if self.part is None else self.buffer.at[index, self.part]

    def first(self):
        own = self.at(self.index)
        self.from_chip = self.copies.start(own, own, self.chip)
        self.from_core = self.copies.start(own, own, self.core)

    def second(self):
        self.from_chip.wait_recv()
        other = self.at((self.index + 2) % RING)
        self.onward = self.copies.start(other, other, self.core)

    def third(self):
        self.from_core.wait_recv()
        self.onward.wait_recv()


def kernel(
    first_flags,
    second_flags,
    sigma,
    panel,
    pivots,
    root_panel,
    parent_panel,
    second_pivots,
    out_sigma_hbm,
    out_diag_hbm,
    out_root_hbm,
    out_parent_hbm,
    out_second_hbm,
    turned,
    blocks,
    sigma_high,
    sigma_low,
    back_high,
    back_low,
    low_group,
    pivot_group,
    parent_all,
    parent_pair,
    lower,
    lower_side,
    reduced,
    reduced_side,
    reduced_pair,
    lower_high,
    lower_low,
    red_high,
    red_low,
    side_high,
    side_low,
    red_side_high,
    red_side_low,
    sum_ay,
    half_ay,
    full_ay,
    sum_az,
    half_az,
    full_az,
    sum_by,
    half_by,
    full_by,
    sum_bz,
    half_bz,
    full_bz,
    cross_turned,
    cross_group,
    sum_f,
    half_f,
    full_f,
    sum_p,
    half_p,
    full_p,
    pivot_parent,
    diag_sum,
    half_d0,
    full_d0,
    half_d1,
    full_d1,
    full_e0,
    full_e1,
    out_sigma,
    out_diag,
    out_root,
    out_parent,
    out_second,
    out_sems,
    send_sems,
    recv_sems,
    local_sems,
):
    row = lax.axis_index("row")
    col = lax.axis_index("col")
    y, z = row // RING, row % RING
    x, core = col // 2, col % 2
    local = col % RING

    def device(at_x, at_core, at_y, at_z):
        return (at_y * RING + at_z, at_x * 2 + at_core)

    def z_device(step):
        return device(x, core, y, (z + step) % RING)

    def y_device(step):
        return device(x, core, (y + step) % RING, z)

    z_plus, z_minus = z_device(1), z_device(3)
    y_plus, y_minus = y_device(1), y_device(3)
    x_plus = device((x + 1) % RING, core, y, z)
    x_minus = device((x + 3) % RING, core, y, z)
    x_pair = device(x + 1 - 2 * (x % 2), core, y, z)
    other_core = device(x, 1 - core, y, z)

    barrier = pltpu.get_barrier_semaphore()
    friends = [y_plus, y_minus, y_device(2), x_plus, x_minus]
    for step in range(RING):
        for flip in range(2):
            if step or flip:
                friends.append(device(x, (core + flip) % 2, y, (z + step) % RING))
    for friend in friends:
        pl.semaphore_signal(barrier, inc=1, device_id=friend, device_id_type=MESH)
    first_flag = first_flags[col // RING, row].astype(F32)
    root_flag = second_flags[x, row].astype(F32)
    parent_flag = second_flags[x, RING * RING + row // 2].astype(F32)
    turned[0] = sigma[:, 0:256].T
    turned[1] = sigma[:, 256:512].T
    parent_lower = parent_panel[...] * parent_flag
    parent_all[y, z] = parent_lower
    parent_pair[core] = parent_lower
    masked = panel[...] * first_flag
    low_group[local] = masked
    lower[z] = masked
    lower_side[y] = masked[:, WIDE:512]
    pl.semaphore_wait(barrier, len(friends))

    copies = Copies(send_sems, recv_sems)
    outputs = []

    parent_y0 = Gather(
        copies, y_plus, y_minus, y,
        lambda i: (parent_all.at[i, z, 0:24], parent_all.at[i, z, 24:48]),
    )
    parent_z1 = Gather(
        copies, z_plus, z_minus, z,
        lambda i: (parent_all.at[y, i, 48:88], parent_all.at[y, i, 88:128]),
    )
    parent_z0 = Gather(
        copies, z_plus, z_minus, z,
        lambda i: (parent_all.at[0:2, i, 0:48], parent_all.at[2:4, i, 0:48]),
    )
    parent_y1 = Gather(
        copies, y_plus, y_minus, y,
        lambda i: (parent_all.at[i, 0:2, 48:128], parent_all.at[i, 2:4, 48:128]),
    )
    parent_y0.first()
    parent_z1.first()

    sigma_send = []
    for j in range(2):
        at_z = core * 2 + j
        copy = pltpu.make_async_remote_copy(
            src_ref=turned.at[j],
            dst_ref=blocks.at[x, z],
            send_sem=local_sems.at[2 + j],
            recv_sem=local_sems.at[z % 2],
            device_id=device(x, z // 2, y, at_z),
            device_id_type=MESH,
        )
        sigma_send.append((at_z, copy))

        @pl.when(at_z != z)
        def _():
            copy.start()

        @pl.when(at_z == z)
        def _():
            blocks[x, z] = turned[j]

    low_gather = Group(copies, x_pair, other_core, local, low_group)
    low_gather.first()

    def over_z(array, start, stop):
        return Gather(
            copies, z_plus, z_minus, z,
            lambda i: (array.at[i, 0:128, start:stop], array.at[i, 128:256, start:stop]),
        )

    def over_y(array):
        return Gather(
            copies, y_plus, y_minus, y,
            lambda i: (array.at[i, 0:128], array.at[i, 128:256]),
        )

    lower_z = over_z(lower, 0, WIDE)
    lower_y = over_y(lower_side)
    lower_rest = over_z(lower, WIDE, 512)
    reduced_z = over_z(reduced, 0, WIDE)
    reduced_y = over_y(reduced_side)
    reduced_rest = over_z(reduced, WIDE, 512)
    pair = parent_pair.at[core]
    pair_copy = copies.start(pair, pair, other_core)
    pivot_group[local] = pivots[...]
    parent_y0.second()
    parent_z1.second()

    for j in range(2):
        from_z = core * 2 + j

        @pl.when(from_z != z)
        def _():
            pltpu.make_async_remote_copy(
                src_ref=turned.at[j],
                dst_ref=blocks.at[x, from_z],
                send_sem=local_sems.at[2 + j],
                recv_sem=local_sems.at[j],
                device_id=other_core,
                device_id_type=MESH,
            ).wait_recv()

    sigma_gather = Gather(
        copies, x_plus, x_minus, x,
        lambda i: (blocks.at[i, 2 * core], blocks.at[i, 2 * core + 1]),
    )
    sigma_gather.first()

    def share(i):
        ref = blocks.at[i, pl.ds(2 * core, 2)]
        return copies.start(ref, ref, other_core)

    def ready(copy, i):
        copy.wait_recv()
        for k in range(RING):
            value = blocks[i, k]
            high, low = split(value)
            sigma_high[i, k] = high
            sigma_low[i, k] = low
            high, low = split(value.T)
            back_high[i, k] = high
            back_low[i, k] = low

    shared = share(x)
    parent_y0.third()
    parent_z0.first()
    parent_z1.third()
    parent_y1.first()
    lower_z.first()
    lower_y.first()
    low_gather.second()
    pivot_gather = Group(copies, x_pair, other_core, local, pivot_group)
    pivot_gather.first()
    ready(shared, x)
    parent_z0.second()
    parent_y1.second()
    lower_z.second()
    lower_y.second()
    sigma_gather.second()
    sigma_gather.near()
    shared_near = [share((x + 1) % RING), share((x + 3) % RING)]
    pivot_gather.second()
    low_gather.third()
    lower_z.third()
    lower_y.third()

    def split_rows(array, high, low, start, stop):
        for i in range(RING):
            high[i, :, start:stop], low[i, :, start:stop] = split(array[i, :, start:stop])

    split_rows(lower, lower_high, lower_low, 0, WIDE)
    split_rows(lower_side, side_high, side_low, 0, 512 - WIDE)
    ready(shared_near[0], (x + 1) % RING)
    ready(shared_near[1], (x + 3) % RING)
    parent_z0.third()
    parent_y1.third()

    total = root_panel[...] * root_flag
    for i in range(RING):
        total -= dot3(split(low_group[i]), split(parent_all[i].reshape(512, 512)))
    reduced[z] = total
    reduced_side[y] = total[:, WIDE:512]
    reduced_pair[core] = total
    reduced_z.first()
    reduced_y.first()
    ref = reduced_pair.at[core]
    reduced_copy = copies.start(ref, ref, other_core)
    sigma_gather.far()
    ready(share((x + 2) % RING), (x + 2) % RING)

    def scatter(plus, minus, index, summed, half_in, full_in, rows):
        return Scatter(
            copies, plus, minus, index,
            lambda i: summed.at[i],
            lambda i: (summed.at[i, 0 : rows // 2], summed.at[i, rows // 2 : rows]),
            half_in, full_in,
            lambda i: (full_in.at[i, 0 : rows // 2], full_in.at[i, rows // 2 : rows]),
        )

    def fill_y(into, at, high, low):
        total = None
        for i in range(RING):
            left = (sigma_high[at, i], sigma_low[at, i])
            term = dot3(left, (high[i, :, 0:WIDE], low[i, :, 0:WIDE]))
            total = term if total is None else total + term
        into[at] = total

    def fill_z(into, at, high, low):
        total = None
        for i in range(RING):
            term = dot3((back_high[i, at], back_low[i, at]), (high[i], low[i]))
            total = term if total is None else total + term
        into[at] = total

    first_y = scatter(y_plus, y_minus, y, sum_ay, half_ay, full_ay, 256)
    first_z = scatter(z_plus, z_minus, z, sum_az, half_az, full_az, 256)
    fill_y(sum_ay, (y + 2) % RING, lower_high, lower_low)
    first_y.first()
    fill_z(sum_az, (z + 2) % RING, side_high, side_low)
    first_z.first()
    reduced_z.second()
    reduced_y.second()
    for step in (1, 3):
        fill_y(sum_ay, (y + step) % RING, lower_high, lower_low)
    first_y.middle()
    first_y.second()
    for step in (1, 3):
        fill_z(sum_az, (z + step) % RING, side_high, side_low)
    first_z.middle()
    first_z.second()
    lower_rest.first()
    fill_y(sum_ay, y, lower_high, lower_low)
    fill_z(sum_az, z, side_high, side_low)
    pivot_gather.third()
    pair_copy.wait_recv()
    total = jnp.zeros((128, 512), F32)
    for i in range(RING):
        total += dot3(split(pivot_group[i]), split(parent_all[i].reshape(512, 512)))
    pivot_parent[...] = total
    right = split(total)
    for k in range(2):
        term = dot3(split(parent_pair[k].T), right)
        diag_sum[2 * k : 2 * k + 2] = term.reshape(2, RING, 64, 512)
    reduced_z.third()
    split_rows(reduced, red_high, red_low, 0, WIDE)
    second_y = scatter(y_plus, y_minus, y, sum_by, half_by, full_by, 256)
    second_z = scatter(z_plus, z_minus, z, sum_bz, half_bz, full_bz, 256)
    fill_y(sum_by, (y + 2) % RING, red_high, red_low)
    cross_copies = []

    def send_cross(scattered, start, stop, output):
        cross = scattered.third() * (-first_flag)
        output[:, start:stop] = cross
        first, last = start // 128, stop // 128
        cross_turned[first:last] = cross.T.reshape(last - first, 128, 256)

    send_cross(first_y, 0, WIDE, out_sigma)
    second_y.first()
    reduced_y.third()
    split_rows(reduced_side, red_side_high, red_side_low, 0, 512 - WIDE)
    fill_z(sum_bz, (z + 2) % RING, red_side_high, red_side_low)
    send_cross(first_z, WIDE, 512, out_sigma)
    outputs.append(pltpu.make_async_copy(out_sigma, out_sigma_hbm, out_sems.at[0]))
    outputs[-1].start()
    cross_group[local, z] = cross_turned[z]
    for step in (1, 3, 2):
        at_z = (z + step) % RING
        cross_copies.append(
            copies.start(cross_turned.at[at_z], cross_group.at[local, z], z_device(step))
        )
    second_z.first()
    cross_gathers = []

    def pass_on(from_z):
        gather = Group(copies, x_pair, other_core, local, cross_group, from_z)
        gather.first()
        cross_gathers.append(gather)

    pass_on(z)
    for step in (1, 3):
        fill_y(sum_by, (y + step) % RING, red_high, red_low)
    second_y.middle()
    second_y.second()
    for copy, step in zip(cross_copies, (1, 3, 2)):
        copy.wait_recv()
        pass_on((z + RING - step) % RING)
    reduced_rest.first()
    for step in (1, 3):
        fill_z(sum_bz, (z + step) % RING, red_side_high, red_side_low)
    second_z.middle()
    second_z.second()
    lower_rest.second()
    fill_y(sum_by, y, red_high, red_low)
    fill_z(sum_bz, z, red_side_high, red_side_low)

    reduced_copy.wait_recv()
    for gather in cross_gathers:
        gather.second()
    lower_rest.third()
    split_rows(lower, lower_high, lower_low, WIDE, 512)

    for scattered, start, stop in ((second_y, 0, WIDE), (second_z, WIDE, 512)):
        result = scattered.third()
        out_root[:, start:stop] = result * (-root_flag)
        right = split(result)
        for k in range(2):
            term = dot3(split(reduced_pair[k].T), right)
            diag_sum[2 * k : 2 * k + 2, :, :, start:stop] += term.reshape(2, RING, 64, stop - start)
    outputs.append(pltpu.make_async_copy(out_root, out_root_hbm, out_sems.at[2]))
    outputs[-1].start()
    diag_y0 = Scatter(
        copies, y_plus, y_minus, y,
        lambda i: diag_sum.at[i, :, :, 0:128],
        lambda i: (diag_sum.at[i, 0:2, :, 0:128], diag_sum.at[i, 2:4, :, 0:128]),
        half_d0, full_d0,
        lambda i: (full_d0.at[i, 0:2], full_d0.at[i, 2:4]),
    )
    diag_z1 = Scatter(
        copies, z_plus, z_minus, z,
        lambda i: diag_sum.at[:, i, :, 128:512],
        lambda i: (diag_sum.at[0:2, i, :, 128:512], diag_sum.at[2:4, i, :, 128:512]),
        half_d1, full_d1,
        lambda i: (full_d1.at[i, 0:2], full_d1.at[i, 2:4]),
    )
    diag_y0.first()
    diag_z1.first()
    diag_y0.middle()
    diag_z1.middle()
    reduced_rest.second()
    for gather in cross_gathers:
        gather.third()

    def node_fill(into, at, high, low):
        total = None
        for i in range(RING):
            term = dot3(split(cross_group[at, i]), (high[i], low[i]))
            total = term if total is None else total + term
        into[at] = total

    node_f = scatter(y_plus, y_minus, y, sum_f, half_f, full_f, 128)
    node_p = scatter(y_plus, y_minus, y, sum_p, half_p, full_p, 128)
    node_fill(sum_f, (y + 2) % RING, lower_high, lower_low)
    node_f.first()
    diag_y0.second()
    diag_z1.second()
    for step in (1, 3):
        node_fill(sum_f, (y + step) % RING, lower_high, lower_low)
    node_f.middle()
    node_f.second()
    reduced_rest.third()
    split_rows(reduced, red_high, red_low, WIDE, 512)
    node_fill(sum_p, (y + 2) % RING, red_high, red_low)
    node_p.first()
    for step in (1, 3):
        node_fill(sum_p, (y + step) % RING, red_high, red_low)
    node_p.middle()
    node_p.second()
    node_fill(sum_f, y, lower_high, lower_low)
    node_fill(sum_p, y, red_high, red_low)
    diag_sum[y, :, :, 0:128] = diag_y0.third()
    diag_z0 = Direct(copies, z_device, z, lambda i: diag_sum.at[y, i, :, 0:128], full_e0)
    diag_z0.first()
    diag_sum[:, z, :, 128:512] = diag_z1.third()
    diag_y1 = Direct(copies, y_device, y, lambda i: diag_sum.at[i, z, :, 128:512], full_e1)
    diag_y1.first()
    out_diag[...] = pivots[...] - node_f.third()
    outputs.append(pltpu.make_async_copy(out_diag, out_diag_hbm, out_sems.at[1]))
    outputs[-1].start()
    out_second[:, 0:128] = second_pivots[:, 0:128] + diag_z0.third()
    out_second[:, 128:512] = second_pivots[:, 128:512] + diag_y1.third()
    outputs.append(pltpu.make_async_copy(out_second, out_second_hbm, out_sems.at[4]))
    outputs[-1].start()
    out_parent[...] = (pivot_parent[...] + node_p.third()) * (-parent_flag)
    outputs.append(pltpu.make_async_copy(out_parent, out_parent_hbm, out_sems.at[3]))
    outputs[-1].start()

    copies.finish()
    for copy in outputs:
        copy.wait()
    for at_z, copy in sigma_send:

        @pl.when(at_z != z)
        def _():
            copy.wait_send()


def hand_over(*refs):
    for result, output in zip(refs[:5], refs[5:]):
        output[...] = result[...]


def per_device(sigma, panel, pivots, root_panel, parent_panel, second_pivots, first_flags, second_flags):
    vmem = pl.BlockSpec(memory_space=pltpu.VMEM)
    smem = pl.BlockSpec(memory_space=pltpu.SMEM)

    def scratch(*shape, dtype=F32):
        return pltpu.VMEM(shape, dtype)

    results = pl.pallas_call(
        kernel,
        out_shape=[
            jax.ShapeDtypeStruct((256, 512), F32),
            jax.ShapeDtypeStruct((128, 512), F32),
            jax.ShapeDtypeStruct((256, 512), F32),
            jax.ShapeDtypeStruct((128, 512), F32),
            jax.ShapeDtypeStruct((64, 512), F32),
        ],
        in_specs=[smem] * 2 + [vmem] * 6,
        out_specs=[pl.BlockSpec(memory_space=pl.ANY)] * 5,
        scratch_shapes=[
            scratch(2, 256, 256),
            scratch(4, 4, 256, 256),
            scratch(4, 4, 256, 256, dtype=BF16),
            scratch(4, 4, 256, 256, dtype=BF16),
            scratch(4, 4, 256, 256, dtype=BF16),
            scratch(4, 4, 256, 256, dtype=BF16),
            scratch(4, 256, 512),
            scratch(4, 128, 512),
            scratch(4, 4, 128, 512),
            scratch(2, 128, 512),
            scratch(4, 256, 512),
            scratch(4, 256, 512 - WIDE),
            scratch(4, 256, 512),
            scratch(4, 256, 512 - WIDE),
            scratch(2, 256, 512),
            scratch(4, 256, 512, dtype=BF16),
            scratch(4, 256, 512, dtype=BF16),
            scratch(4, 256, 512, dtype=BF16),
            scratch(4, 256, 512, dtype=BF16),
            scratch(4, 256, 512 - WIDE, dtype=BF16),
            scratch(4, 256, 512 - WIDE, dtype=BF16),
            scratch(4, 256, 512 - WIDE, dtype=BF16),
            scratch(4, 256, 512 - WIDE, dtype=BF16),
            scratch(4, 256, WIDE),
            scratch(2, 128, WIDE),
            scratch(2, 256, WIDE),
            scratch(4, 256, 512 - WIDE),
            scratch(2, 128, 512 - WIDE),
            scratch(2, 256, 512 - WIDE),
            scratch(4, 256, WIDE),
            scratch(2, 128, WIDE),
            scratch(2, 256, WIDE),
            scratch(4, 256, 512 - WIDE),
            scratch(2, 128, 512 - WIDE),
            scratch(2, 256, 512 - WIDE),
            scratch(4, 128, 256),
            scratch(4, 4, 128, 256),
            scratch(4, 128, 512),
            scratch(2, 64, 512),
            scratch(2, 128, 512),
            scratch(4, 128, 512),
            scratch(2, 64, 512),
            scratch(2, 128, 512),
            scratch(128, 512),
            scratch(4, 4, 64, 512),
            scratch(2, 2, 64, 128),
            scratch(2, 4, 64, 128),
            scratch(2, 2, 64, 384),
            scratch(2, 4, 64, 384),
            scratch(3, 64, 128),
            scratch(3, 64, 384),
            scratch(256, 512),
            scratch(128, 512),
            scratch(256, 512),
            scratch(128, 512),
            scratch(64, 512),
            pltpu.SemaphoreType.DMA((5,)),
            pltpu.SemaphoreType.DMA((SENDS,)),
            pltpu.SemaphoreType.DMA((COPIES,)),
            pltpu.SemaphoreType.DMA((4,)),
        ],
        compiler_params=pltpu.CompilerParams(
            collective_id=0, has_side_effects=True, vmem_limit_bytes=60 * 1024 * 1024
        ),
        cost_estimate=pl.CostEstimate(flops=13_000_000_000, bytes_accessed=4_000_000, transcendentals=0),
    )(first_flags, second_flags, sigma, panel, pivots, root_panel, parent_panel, second_pivots)
    return pl.pallas_call(
        hand_over,
        out_shape=[jax.ShapeDtypeStruct(r.shape, r.dtype) for r in results],
        in_specs=[vmem] * 5,
        out_specs=[vmem] * 5,
    )(*results)


def solution(mesh):
    split_both = P("row", "col")
    return jax.shard_map(
        per_device,
        mesh=mesh,
        in_specs=(split_both,) * 6 + (P(), P()),
        out_specs=(split_both,) * 5,
        check_vma=False,
    )
```
